32 devices in a mesh: date: 4 (over z), az: 8 (over y, x, core).
Axes of the slice: x: 2, y: 2, z: 4, core: 2. Of those that a mesh axis runs over, the one named last changes fastest.
Arguments:
- slc_stack: bfloat16 [2, 256, 256, 128], P(None, 'date', 'az'), may hold values from -6 to 6
- fir_taps: float32 [256, 5], P('date'), may hold values from 0.1 to 1
- look_index: int32 [8, 4, 64], P('az', 'date'), may hold values from 0 to 1023
- shrink_level: int32 [8, 4], P('az', 'date'), may hold values from 1 to 12
- window_half: int32 [256], replicated, may hold values from 0 to 2
- basis: bfloat16 [32, 256], replicated, may hold values from -0.375 to 0.375
Outputs:
- projection: float32 [32, 2, 256, 128], P('date', None, 'az')
The draws below stay inside these ranges and needn't reach their ends.
Inputs may be any that keep to these rules, and one draw needn't show every extreme that they name: `look_index`: pixel numbers inside one block of 8 rows.
All inputs are finite; a program needn't handle non-finite values.
Results may differ from the reference program's by a relative error of at most 0.0048.
Values may be sent and summed in bfloat16 or wider, within the bound.
A program may use at most 64 MiB of HBM per device.

```python
import jax
import jax.numpy as jnp
from jax import lax

DATES = 256
BASES = 32
LOOKS = 64
NS_ITERS = 6
FIR_REACH = 2
SMOOTH_REACH = 2
RG = 128
PIX_DEV = 1024
TAPS = 5
BLOCK_ROWS = 8
AZ = 256
N_DATE = 4
N_AZ = 8


def touch_ends(entries, rng, least, largest):
    place = [jax.random.randint(jax.random.fold_in(rng, axis), (), 0, length) for axis, length in enumerate(entries.shape)]
    main_axis = entries.shape.index(max(entries.shape))
    neighbour = place[:main_axis] + [(place[main_axis] + 1) % entries.shape[main_axis]] + place[main_axis + 1:]
    return entries.at[tuple(place)].set(least).at[tuple(neighbour)].set(largest)


def shard_levels(rng, extent, split, smallest, top_value):
    level = 1.0
    for dim, blocks in split:
        steps = jax.random.uniform(jax.random.fold_in(jax.random.fold_in(rng, 6), dim), (blocks,), jnp.float32, smallest / len(split), top_value / len(split))
        level = level * jnp.repeat(jnp.exp(steps), extent[dim] // blocks).reshape((-1,) + (1,) * (len(extent) - 1 - dim))
    return level


def normal_values(rng, shape, width, most, split=(), held_as=jnp.bfloat16):
    level = shard_levels(rng, shape, split, -0.22, 0.18) if split else 1.0
    values = jax.random.normal(rng, shape, jnp.float32) * width * level
    return jnp.minimum(jnp.maximum(values, -most), most).astype(held_as)


def setup_inputs(seed: int = 0) -> dict:
    seeds = jax.random.split(jax.random.key(seed), 7)
    slc_stack = normal_values(seeds[0], (2, DATES, AZ, RG), 1.0, 6.0, ((1, 4), (2, 8)))
    fir_taps = jnp.clip(0.1 + 0.9 * jax.random.uniform(seeds[1], (DATES, TAPS), jnp.float32) ** shard_levels(seeds[1], (DATES, TAPS), ((0, 4),), -0.2, 0.2), 0.1, 1.0)
    look_index = touch_ends(jax.random.randint(seeds[2], (N_AZ, N_DATE, LOOKS), 0, PIX_DEV), jax.random.fold_in(seeds[2], 1), 0, PIX_DEV - 1).astype(jnp.int32)
    shrink_level = touch_ends(jax.random.randint(seeds[3], (N_AZ, N_DATE), 1, 13), jax.random.fold_in(seeds[3], 1), 1, 12).astype(jnp.int32)
    window_half = touch_ends(jax.random.randint(seeds[4], (DATES,), 0, SMOOTH_REACH + 1), jax.random.fold_in(seeds[4], 1), 0, SMOOTH_REACH).astype(jnp.int32)
    basis = normal_values(seeds[5], (BASES, DATES), DATES ** -0.5, 0.375)
    return dict(slc_stack=slc_stack, fir_taps=fir_taps, look_index=look_index, shrink_level=shrink_level, window_half=window_half, basis=basis)


def complex_product(left_re, left_im, right_re, right_im):
    highest = lax.Precision.HIGHEST
    real = jnp.dot(left_re, right_re, precision=highest) - jnp.dot(left_im, right_im, precision=highest)
    imag = jnp.dot(left_re, right_im, precision=highest) + jnp.dot(left_im, right_re, precision=highest)
    return (real, imag)

def wiener_block(pixels, chosen, level):
    sample = jnp.take(pixels, chosen, axis=2)
    samp_re = sample[0]
    samp_im = sample[1]
    looks = chosen.shape[0]
    gram_re = (jnp.dot(samp_re, samp_re.T, preferred_element_type=jnp.float32) + jnp.dot(samp_im, samp_im.T, preferred_element_type=jnp.float32)) / looks
    gram_im = (jnp.dot(samp_im, samp_re.T, preferred_element_type=jnp.float32) - jnp.dot(samp_re, samp_im.T, preferred_element_type=jnp.float32)) / looks
    count = gram_re.shape[0]
    identity = jnp.eye(count, dtype=jnp.float32)
    level_mean = jnp.trace(gram_re) / count + 1e-06
    weight = level.astype(jnp.float32) / 16.0
    shrunk_re = (1.0 - weight) * gram_re + weight * level_mean * identity
    shrunk_im = (1.0 - weight) * gram_im
    load_re = shrunk_re + level_mean * identity
    load_im = shrunk_im
    scale = 1.0 / jnp.sqrt(jnp.sum(load_re * load_re + load_im * load_im))
    inv_re = identity * scale
    inv_im = jnp.zeros_like(identity)
    for step in range(NS_ITERS):
        prod_re, prod_im = complex_product(load_re, load_im, inv_re, inv_im)
        inv_re, inv_im = complex_product(inv_re, inv_im, 2.0 * identity - prod_re, -prod_im)
    gain_re, gain_im = complex_product(shrunk_re, shrunk_im, inv_re, inv_im)
    gain_re = gain_re.astype(jnp.bfloat16)
    gain_im = gain_im.astype(jnp.bfloat16)
    pix_re = pixels[0]
    pix_im = pixels[1]
    out_re = jnp.dot(gain_re, pix_re, preferred_element_type=jnp.float32) - jnp.dot(gain_im, pix_im, preferred_element_type=jnp.float32)
    out_im = jnp.dot(gain_re, pix_im, preferred_element_type=jnp.float32) + jnp.dot(gain_im, pix_re, preferred_element_type=jnp.float32)
    return jnp.stack([out_re, out_im]).astype(jnp.bfloat16)

def smooth_weights(halves, reach):
    offsets = jnp.arange(-reach, reach + 1)
    inside = (jnp.abs(offsets)[None, :] <= halves[:, None]).astype(jnp.float32)
    return inside / (2 * halves + 1).astype(jnp.float32)[:, None]

def reference(slc_stack, fir_taps, look_index, shrink_level, window_half, basis):
    rows = slc_stack.shape[2]
    padded = jnp.pad(slc_stack.astype(jnp.float32), ((0, 0), (0, 0), (FIR_REACH, FIR_REACH), (0, 0)))
    filtered = jnp.zeros(slc_stack.shape, jnp.float32)
    for offset in range(TAPS):
        filtered = filtered + fir_taps[:, offset][None, :, None, None] * padded[:, :, offset:offset + rows, :]
    filtered = filtered.astype(jnp.bfloat16)
    blocks = rows // BLOCK_ROWS
    grouped = filtered.reshape(2, DATES, blocks, PIX_DEV).transpose(2, 0, 1, 3)
    chosen_all = look_index.reshape(blocks, LOOKS).astype(jnp.int32)
    levels = shrink_level.reshape(blocks).astype(jnp.int32)
    wiener = lax.map(lambda item: wiener_block(item[0], item[1], item[2]), (grouped, chosen_all, levels))
    wiener = wiener.transpose(1, 2, 0, 3).reshape(2, DATES, rows, RG)
    weights = smooth_weights(window_half, SMOOTH_REACH)
    rim = jnp.pad(wiener.astype(jnp.float32), ((0, 0), (0, 0), (SMOOTH_REACH, SMOOTH_REACH), (0, 0)))
    smoothed = jnp.zeros(wiener.shape, jnp.float32)
    for offset in range(2 * SMOOTH_REACH + 1):
        smoothed = smoothed + weights[:, offset][None, :, None, None] * rim[:, :, offset:offset + rows, :]
    smoothed = smoothed.astype(jnp.bfloat16)
    return jnp.einsum('kt,ctrg->kcrg', basis.astype(jnp.float32), smoothed.astype(jnp.float32), precision=lax.Precision.HIGHEST)
```

```python
import functools

import jax
import jax.numpy as jnp
import numpy as np
from jax import lax
from jax.experimental import pallas as pl
from jax.experimental.pallas import tpu as pltpu
from jax.sharding import PartitionSpec as P

NS_ITERS = 6
SMOOTH_REACH = 2
MESH = pl.DeviceIdType.MESH
HIGHEST = lax.Precision.HIGHEST
F32 = jnp.float32
BF16 = jnp.bfloat16


def exact_dot(left, right):
    return jnp.dot(left, right, precision=HIGHEST, preferred_element_type=F32)


def project_gain(what, weight, masked, scales, looks):
    dates2, width = what.shape
    dates = dates2 // 2
    gram = lax.dot_general(what, what, (((0,), (0,)), ((), ())), preferred_element_type=F32)
    line = lax.broadcasted_iota(jnp.int32, (width, width), 0)
    column = lax.broadcasted_iota(jnp.int32, (width, width), 1)
    eye = (line == column).astype(F32)

    def total(array):
        return jnp.sum(jnp.sum(array, axis=1, keepdims=True), axis=0, keepdims=True)

    trace = total(gram * eye) * 0.5
    mu = trace / (looks * dates) + 1e-06
    alpha = (1.0 - weight) / looks
    c = (1.0 + weight) * mu
    core = alpha * gram
    square = total(core * core) * 0.5 + 2.0 * c * alpha * trace + c * c * dates
    scale = 1.0 / jnp.sqrt(square)
    rho = 1.0 - scale * c
    r = rho * eye - scale * core
    first = r
    dr = -scale * (rho * eye + first)
    df = -scale * eye
    f0 = 1.0 + rho
    r = exact_dot(first, first)
    rho = rho * rho
    for step in range(1, NS_ITERS):
        if step == NS_ITERS - 1:
            df = f0 * dr + df + exact_dot(df, r)
            f0 = f0 * (1.0 + rho)
        elif step == 1:
            out = exact_dot(jnp.concatenate([dr, r], axis=0), r)
            df = f0 * dr + df - scale * r
            f0 = f0 * (1.0 + rho)
            dr = rho * dr + out[:width]
            r = out[width:]
            rho = rho * rho
        else:
            out = exact_dot(jnp.concatenate([df, dr, r], axis=0), r)
            df = f0 * dr + df + out[:width]
            f0 = f0 * (1.0 + rho)
            dr = rho * dr + out[width : 2 * width]
            r = out[2 * width :]
            rho = rho * rho
    inner = scale * (f0 * eye + weight * mu * df + exact_dot(core, df))
    base = weight * mu * scale * f0
    seen = lax.dot_general(what[:dates], masked, (((0,), (1,)), ((), ())), preferred_element_type=F32)
    small = exact_dot(inner, alpha * seen)
    both = exact_dot(what.astype(F32), small)
    real = (both[:dates] + base * jnp.transpose(masked.astype(F32))) * scales
    imag = both[dates:] * scales
    return real.astype(BF16), imag.astype(BF16)


def kernel(
    groups, slabs, looks, taps_count, unit,
    x_ref, taps_ref, idx_ref, weight_ref, masked_ref, scales_ref, order_ref, out_ref,
    halo, idx_all, z, wsend, what, vsend, vrecv, u, psend, precv, esend, erecv,
    s_halo, r_halo, s_idx, r_idx, s_w, r_w, s_v, r_v, s_p, r_p, s_e, r_e,
):
    me = lax.axis_index("date")
    az = lax.axis_index("az")
    rows, dates2, cols = x_ref.shape
    dates = dates2 // 2
    block_rows = rows // groups
    reach = taps_count // 2
    classes = SMOOTH_REACH + 1
    has_low = az > 0
    has_high = az < slabs - 1

    barrier = pltpu.get_barrier_semaphore()
    peers = [lax.rem(me + o, groups) for o in range(groups)]

    def greet(d, a):
        pl.semaphore_signal(barrier, inc=1, device_id={"date": d, "az": a}, device_id_type=MESH)

    for o in range(1, groups):
        greet(peers[o], az)

    @pl.when(has_low)
    def _():
        for o in range(groups):
            greet(peers[o], az - 1)

    @pl.when(has_high)
    def _():
        for o in range(groups):
            greet(peers[o], az + 1)

    pl.semaphore_wait(
        barrier,
        groups - 1 + groups * (has_low.astype(jnp.int32) + has_high.astype(jnp.int32)),
    )

    def remote(src, dst, send, recv, d, a):
        return pltpu.make_async_remote_copy(
            src_ref=src, dst_ref=dst, send_sem=send, recv_sem=recv,
            device_id={"date": d, "az": a}, device_id_type=MESH,
        )

    def halo_down():
        return remote(x_ref.at[pl.ds(0, reach)], halo.at[1], s_halo.at[0], r_halo.at[1], me, az - 1)

    def halo_up():
        return remote(
            x_ref.at[pl.ds(rows - reach, reach)], halo.at[0], s_halo.at[1], r_halo.at[0], me, az + 1
        )

    def idx_copy(o, src):
        return remote(idx_ref, idx_all.at[src], s_idx.at[o], r_idx.at[src], peers[o], az)

    pl.when(has_low)(lambda: halo_down().start())
    pl.when(has_high)(lambda: halo_up().start())
    for o in range(1, groups):
        idx_copy(o, me).start()
    idx_all[me] = idx_ref[...]

    def fir(b, i, row_of):
        total = None
        for j in range(taps_count):
            term = taps_ref[:, j : j + 1] * row_of(i + j - reach).astype(F32)
            total = term if total is None else total + term
        z[b, :, i * cols : (i + 1) * cols] = total.astype(BF16)

    @pl.loop(0, groups)
    def _(b):
        for i in range(block_rows):
            if reach <= i < block_rows - reach:
                fir(b, i, lambda q: x_ref[b * block_rows + q])

    @pl.loop(0, groups - 1)
    def _(b):
        for i in range(block_rows - reach, block_rows):
            fir(b, i, lambda q: x_ref[b * block_rows + q])
        for i in range(reach):
            fir(b + 1, i, lambda q: x_ref[(b + 1) * block_rows + q])

    @pl.when(has_low)
    def _():
        halo_up().wait_recv()

    @pl.when(jnp.logical_not(has_low))
    def _():
        halo[0] = jnp.zeros(halo.shape[1:], BF16)

    @pl.when(has_high)
    def _():
        halo_down().wait_recv()

    @pl.when(jnp.logical_not(has_high))
    def _():
        halo[1] = jnp.zeros(halo.shape[1:], BF16)

    for i in range(reach):
        fir(0, i, lambda q: x_ref[q] if q >= 0 else halo[0, reach + q])
    last = (groups - 1) * block_rows
    for i in range(block_rows - reach, block_rows):
        fir(
            groups - 1, i,
            lambda q: x_ref[last + q] if q < block_rows else halo[1, q - block_rows],
        )

    def w_copy(o, src):
        return remote(
            wsend.at[peers[o]],
            what.at[:, pl.ds(pl.multiple_of(src * dates, dates), dates), :],
            s_w.at[o], r_w.at[src], peers[o], az,
        )

    for o in list(range(1, groups)) + [0]:
        b = peers[o]
        if o:
            idx_copy(o, b).wait_recv()
        chosen = idx_all[b][0:1, :]
        pixel = lax.broadcasted_iota(jnp.int32, (block_rows * cols, 2 * looks), 0)
        pick = (pixel == chosen).astype(F32).astype(BF16)
        sample = jnp.dot(z[b], pick, preferred_element_type=F32)
        left = lax.broadcasted_iota(jnp.int32, (dates, 2 * looks), 1) < looks
        real, imag = sample[:dates], sample[dates:]
        top = jnp.where(left, real, -imag).astype(BF16)
        bottom = jnp.where(left, imag, real).astype(BF16)
        if o:
            wsend[b, 0] = top
            wsend[b, 1] = bottom
            w_copy(o, me).start()
        else:
            own = pl.ds(pl.multiple_of(me * dates, dates), dates)
            what[0, own, :] = top
            what[1, own, :] = bottom
    for o in range(1, groups):
        w_copy(o, peers[o]).wait_recv()

    whole = what[...].reshape(2 * groups * dates, 2 * looks)
    real, imag = project_gain(whole, weight_ref[0:1, 0:1], masked_ref[...], scales_ref[0:1, :], looks)
    vsend[0] = real
    vsend[1] = imag

    def v_copy(o, src):
        return remote(
            vsend.at[:, pl.ds(pl.multiple_of(peers[o] * dates, dates), dates), :],
            vrecv.at[src], s_v.at[o], r_v.at[src], peers[o], az,
        )

    for o in range(1, groups):
        v_copy(o, me).start()
    vrecv[me] = vsend[:, pl.ds(pl.multiple_of(me * dates, dates), dates), :]

    zeros = jnp.zeros((SMOOTH_REACH,) + u.shape[1:], F32)
    u[0:SMOOTH_REACH] = zeros
    u[rows + SMOOTH_REACH : rows + 2 * SMOOTH_REACH] = zeros
    for o in range(groups):
        b = peers[o]
        if o:
            v_copy(o, b).wait_recv()
        v_re = vrecv[b, 0]
        v_im = vrecv[b, 1]
        upper = jnp.concatenate([v_re, v_im], axis=0)
        lower = jnp.concatenate([-v_im, v_re], axis=0)
        mix = lax.dot_general(
            order_ref[...], jnp.concatenate([upper, lower], axis=1),
            (((1,), (1,)), ((), ())), preferred_element_type=F32,
        ).astype(BF16)
        found = jnp.dot(mix, z[b], preferred_element_type=F32)
        for i in range(block_rows):
            u[SMOOTH_REACH + b * block_rows + i] = found[:, i * cols : (i + 1) * cols]

    def smooth(r, d, place):
        total = None
        for h in range(classes):
            at = pl.ds(pl.multiple_of((h * groups + d) * unit, 8), unit)
            for j in range(-h, h + 1):
                if place is None or 0 <= place + j < rows:
                    term = u[r + j + SMOOTH_REACH, at, :]
                    total = term if total is None else total + term
        return total

    def e_copy(side, o, src, target):
        return remote(
            esend.at[side, peers[o]], erecv.at[1 - side, src],
            s_e.at[side, o], r_e.at[1 - side, src], peers[o], target,
        )

    for o in range(groups):
        d = peers[o]
        for i in range(SMOOTH_REACH):
            esend[0, d, i] = smooth(i - SMOOTH_REACH, d, i - SMOOTH_REACH).astype(BF16)
            esend[1, d, i] = smooth(rows + i, d, rows + i).astype(BF16)
        pl.when(has_low)(lambda o=o: e_copy(0, o, me, az - 1).start())
        pl.when(has_high)(lambda o=o: e_copy(1, o, me, az + 1).start())

    def p_copy(o, src):
        return remote(psend.at[peers[o]], precv.at[src], s_p.at[o], r_p.at[src], peers[o], az)

    for o in range(1, groups):
        d = peers[o]

        @pl.loop(0, rows)
        def _(r):
            psend[d, r] = smooth(r, d, None).astype(BF16)

        p_copy(o, me).start()

    @pl.loop(0, rows)
    def _(r):
        out_ref[r] = smooth(r, me, None)

    @pl.when(has_low)
    def _():
        for o in range(groups):
            e_copy(1, o, peers[o], az - 1).wait_recv()
        for i in range(SMOOTH_REACH):
            for o in range(groups):
                out_ref[i] += erecv[0, peers[o], i].astype(F32)

    @pl.when(has_high)
    def _():
        for o in range(groups):
            e_copy(0, o, peers[o], az + 1).wait_recv()
        for i in range(SMOOTH_REACH):
            for o in range(groups):
                out_ref[rows - SMOOTH_REACH + i] += erecv[1, peers[o], i].astype(F32)

    for o in range(1, groups):
        p_copy(o, peers[o]).wait_recv()
        out_ref[...] += precv[peers[o]].astype(F32)

    pl.when(has_low)(lambda: halo_down().wait_send())
    pl.when(has_high)(lambda: halo_up().wait_send())
    for o in range(groups):
        if o:
            idx_copy(o, me).wait_send()
            w_copy(o, me).wait_send()
            v_copy(o, me).wait_send()
            p_copy(o, me).wait_send()
        pl.when(has_low)(lambda o=o: e_copy(0, o, me, az - 1).wait_send())
        pl.when(has_high)(lambda o=o: e_copy(1, o, me, az + 1).wait_send())


def on_device(slc_stack, fir_taps, look_index, shrink_level, window_half, basis):
    parts, dates, rows, cols = slc_stack.shape
    groups = lax.axis_size("date")
    slabs = lax.axis_size("az")
    taps_count = fir_taps.shape[1]
    looks = look_index.shape[2]
    bases, all_dates = basis.shape
    own = bases // groups
    unit = -(-2 * own // 8) * 8
    classes = SMOOTH_REACH + 1

    x = slc_stack.transpose(2, 0, 1, 3).reshape(rows, parts * dates, cols)
    taps = jnp.concatenate([fir_taps, fir_taps], axis=0)
    chosen = look_index.reshape(1, looks)
    chosen = jnp.broadcast_to(jnp.concatenate([chosen, chosen], axis=1), (8, 2 * looks))
    weight = jnp.broadcast_to(shrink_level.astype(F32) / 16.0, (8, 128))
    inside = window_half[None, :] == jnp.arange(classes)[:, None]
    masked = jnp.where(inside[:, None, :], basis[None], jnp.zeros_like(basis)[None])
    masked = masked.reshape(classes * bases, all_dates)
    filled = -(-masked.shape[0] // 128) * 128
    masked = jnp.pad(masked, ((0, filled - masked.shape[0]), (0, 0)))
    scales = jnp.repeat(1.0 / (2.0 * jnp.arange(classes, dtype=F32) + 1.0), bases)
    scales = jnp.broadcast_to(jnp.pad(scales, (0, filled - scales.shape[0])), (8, filled))
    order_rows = np.zeros((classes, groups, unit, 2, filled), np.float32)
    for h in range(classes):
        for d in range(groups):
            for part in range(2):
                for k in range(own):
                    order_rows[h, d, part * own + k, part, h * bases + d * own + k] = 1.0
    order_rows = jnp.asarray(order_rows.reshape(classes * groups * unit, 2 * filled), BF16)

    block_rows = rows // groups
    dma = pltpu.SemaphoreType.DMA
    vmem = pl.BlockSpec(memory_space=pltpu.VMEM)
    scratch = [
        pltpu.VMEM((2, taps_count // 2, 2 * dates, cols), BF16),
        pltpu.VMEM((groups, 8, 2 * looks), jnp.int32),
        pltpu.VMEM((groups, 2 * dates, block_rows * cols), BF16),
        pltpu.VMEM((groups, 2, dates, 2 * looks), BF16),
        pltpu.VMEM((2, all_dates, 2 * looks), BF16),
        pltpu.VMEM((2, all_dates, filled), BF16),
        pltpu.VMEM((groups, 2, dates, filled), BF16),
        pltpu.VMEM((rows + 2 * SMOOTH_REACH, classes * groups * unit, cols), F32),
        pltpu.VMEM((groups, rows, unit, cols), BF16),
        pltpu.VMEM((groups, rows, unit, cols), BF16),
        pltpu.VMEM((2, groups, SMOOTH_REACH, unit, cols), BF16),
        pltpu.VMEM((2, groups, SMOOTH_REACH, unit, cols), BF16),
        dma((2,)), dma((2,)),
        dma((groups,)), dma((groups,)),
        dma((groups,)), dma((groups,)),
        dma((groups,)), dma((groups,)),
        dma((groups,)), dma((groups,)),
        dma((2, groups)), dma((2, groups)),
    ]
    out = pl.pallas_call(
        functools.partial(kernel, groups, slabs, looks, taps_count, unit),
        out_shape=jax.ShapeDtypeStruct((rows, unit, cols), F32),
        in_specs=[vmem] * 7,
        out_specs=vmem,
        scratch_shapes=scratch,
        compiler_params=pltpu.CompilerParams(
            collective_id=0, has_side_effects=True, vmem_limit_bytes=60 * 2**20
        ),
    )(x, taps, chosen, weight, masked, scales, order_rows)
    out = out[:, : 2 * own].reshape(rows, 2, own, cols)
    return out.transpose(2, 1, 0, 3)


def solution(mesh):
    in_specs = (
        P(None, "date", "az", None),
        P("date", None),
        P("az", "date", None),
        P("az", "date"),
        P(),
        P(),
    )
    out_specs = P("date", None, "az", None)
    return jax.shard_map(
        on_device, mesh=mesh, in_specs=in_specs, out_specs=out_specs, check_vma=False
    )
```

```python
import functools

import jax
import jax.numpy as jnp
from jax import lax
from jax.experimental import pallas as pl
from jax.experimental.pallas import tpu as pltpu
from jax.sharding import PartitionSpec as P

NS_ITERS = 6
SMOOTH_REACH = 2
MESH = pl.DeviceIdType.MESH
HIGHEST = lax.Precision.HIGHEST
F32 = jnp.float32
BF16 = jnp.bfloat16


def exact_dot(left, right):
    return jnp.dot(left, right, precision=HIGHEST, preferred_element_type=F32)


def split_dot(left, right):
    high = right.astype(BF16)
    low = (right - high.astype(F32)).astype(BF16)
    both = lax.dot_general(
        left, jnp.concatenate([high, low], axis=0), (((1,), (1,)), ((), ())),
        preferred_element_type=F32,
    )
    return both[:, : right.shape[0]] + both[:, right.shape[0] :]


def project_gain(what, weight, masked, turned, scales, looks):
    dates2, width = what.shape
    dates = dates2 // 2
    gram = lax.dot_general(what, what, (((0,), (0,)), ((), ())), preferred_element_type=F32)
    line = lax.broadcasted_iota(jnp.int32, (width, width), 0)
    column = lax.broadcasted_iota(jnp.int32, (width, width), 1)
    eye = (line == column).astype(F32)
    left = lax.broadcasted_iota(jnp.int32, (looks, width), 1) < looks

    def total(array):
        return jnp.sum(jnp.sum(array, axis=1, keepdims=True), axis=0, keepdims=True)

    def full(top):
        turn = pltpu.roll(top, looks, 1)
        return jnp.concatenate([top, jnp.where(left, -turn, turn)], axis=0)

    trace = total(gram * eye) * 0.5
    norm = total(gram * gram) * 0.5
    mu = trace / (looks * dates) + 1e-06
    alpha = (1.0 - weight) / looks
    c = (1.0 + weight) * mu
    core = alpha * gram
    square = alpha * alpha * norm + 2.0 * c * alpha * trace + c * c * dates
    scale = 1.0 / jnp.sqrt(square)
    rho = 1.0 - scale * c
    whole = rho * eye - scale * core
    eye = eye[:looks]
    r = whole[:looks]
    dr = -scale * (rho * eye + r)
    df = -scale * eye
    f0 = 1.0 + rho
    r = exact_dot(r, whole)
    rho = rho * rho
    for step in range(1, NS_ITERS):
        whole = full(r)
        if step == NS_ITERS - 1:
            df = f0 * dr + df + exact_dot(df, whole)
            f0 = f0 * (1.0 + rho)
        elif step == 1:
            out = exact_dot(jnp.concatenate([dr, r], axis=0), whole)
            df = f0 * dr + df - scale * r
            f0 = f0 * (1.0 + rho)
            dr = rho * dr + out[:looks]
            r = out[looks:]
            rho = rho * rho
        else:
            out = exact_dot(jnp.concatenate([df, dr, r], axis=0), whole)
            df = f0 * dr + df + out[:looks]
            f0 = f0 * (1.0 + rho)
            dr = rho * dr + out[looks : 2 * looks]
            r = out[2 * looks :]
            rho = rho * rho
    inner = full(scale * (f0 * eye + weight * mu * df + exact_dot(df, core)))
    base = weight * mu * scale * f0
    seen = jnp.dot(masked, what[:dates], preferred_element_type=F32)
    small = exact_dot(alpha * seen, inner)
    both = split_dot(what, small)
    real = (both[:dates] + base * turned) * scales
    imag = both[dates:] * scales
    return real.astype(BF16), imag.astype(BF16)


def kernel(
    groups, slabs, unit, own, pitch, filled,
    x_ref, taps_ref, look_ref, level_ref, window_ref, basis_ref, out_ref,
    xf, halo_send, halo, idx_send, idx_all, masked_ref, turned_ref, order_ref,
    z, wsend, what, vsend, vrecv, u, psend, precv, esend, erecv,
    s_halo, r_halo, s_idx, r_idx, s_w, r_w, s_v, r_v, s_p, r_p, s_e, r_e,
):
    me = lax.axis_index("date")
    az = lax.axis_index("az")
    _, dates, rows, cols = x_ref.shape
    taps_count = taps_ref.shape[1]
    looks = look_ref.shape[1]
    bases = basis_ref.shape[0]
    block_rows = rows // groups
    reach = taps_count // 2
    classes = SMOOTH_REACH + 1
    has_low = az > 0
    has_high = az < slabs - 1

    barrier = pltpu.get_barrier_semaphore()
    peers = [lax.rem(me + o, groups) for o in range(groups)]

    def greet(d, a):
        pl.semaphore_signal(barrier, inc=1, device_id={"date": d, "az": a}, device_id_type=MESH)

    for o in range(1, groups):
        greet(peers[o], az)

    @pl.when(has_low)
    def _():
        for o in range(groups):
            greet(peers[o], az - 1)

    @pl.when(has_high)
    def _():
        for o in range(groups):
            greet(peers[o], az + 1)

    chosen = jnp.broadcast_to(look_ref[...], (8, looks))
    idx_send[...] = jnp.concatenate([chosen, chosen], axis=1)

    def widen(t):
        for part in range(2):
            at = pl.ds(pl.multiple_of((part * dates + t) * pitch, 8), rows)
            xf[at, :] = x_ref[part, t].astype(F32)

    @pl.loop(0, dates // 8)
    def _(g):
        for t in range(8):
            widen(g * 8 + t)

    def fir_rows(part, g):
        first = part * dates + g * 16
        return (
            pl.ds(pl.multiple_of(first, 16), 16),
            lambda r: xf[pl.ds(first * pitch + r, 16, stride=pitch), :],
        )

    @pl.loop(0, dates // 16)
    def _(g):
        for part in range(2):
            at, row = fir_rows(part, g)
            for q in range(reach):
                halo_send[0, q, at, :] = row(q).astype(BF16)
                halo_send[1, q, at, :] = row(rows - reach + q).astype(BF16)

    pl.semaphore_wait(
        barrier,
        groups - 1 + groups * (has_low.astype(jnp.int32) + has_high.astype(jnp.int32)),
    )

    def remote(src, dst, send, recv, d, a):
        return pltpu.make_async_remote_copy(
            src_ref=src, dst_ref=dst, send_sem=send, recv_sem=recv,
            device_id={"date": d, "az": a}, device_id_type=MESH,
        )

    def halo_down():
        return remote(halo_send.at[0], halo.at[1], s_halo.at[0], r_halo.at[1], me, az - 1)

    def halo_up():
        return remote(halo_send.at[1], halo.at[0], s_halo.at[1], r_halo.at[0], me, az + 1)

    def idx_copy(o, src):
        return remote(idx_send, idx_all.at[src], s_idx.at[o], r_idx.at[src], peers[o], az)

    pl.when(has_low)(lambda: halo_down().start())
    pl.when(has_high)(lambda: halo_up().start())
    for o in range(1, groups):
        idx_copy(o, me).start()
    idx_all[me] = idx_send[...]

    def taps_of(g):
        taps = taps_ref[pl.ds(pl.multiple_of(g * 16, 16), 16), :]
        return [jnp.broadcast_to(taps[:, j : j + 1], (16, cols)) for j in range(taps_count)]

    def fir(r, at, taps, window):
        total = taps[0] * window[0]
        for j in range(1, taps_count):
            total = total + taps[j] * window[j]
        b, i = r // block_rows, r % block_rows
        z[b, at, i * cols : (i + 1) * cols] = total.astype(BF16)

    @pl.loop(0, dates // 16)
    def _(g):
        taps = taps_of(g)
        for part in range(2):
            at, row = fir_rows(part, g)
            window = [row(r) for r in range(2 * reach)]
            for r in range(reach, rows - reach):
                window = window[-2 * reach :] + [row(r + reach)]
                fir(r, at, taps, window)

    zeros = jnp.zeros((SMOOTH_REACH,) + u.shape[1:], F32)
    u[0:SMOOTH_REACH] = zeros
    u[rows + SMOOTH_REACH : rows + 2 * SMOOTH_REACH] = zeros
    basis = basis_ref[...].astype(F32)
    masked = [jnp.where(window_ref[...] == h, basis, 0.0) for h in range(classes)]
    if filled > classes * bases:
        masked.append(jnp.zeros((filled - classes * bases, basis.shape[1]), F32))
    masked = jnp.concatenate(masked, axis=0)
    masked_ref[...] = masked.astype(BF16)
    turned_ref[...] = jnp.transpose(masked)
    lane = lax.broadcasted_iota(jnp.int32, (1, filled), 1)
    scales = jnp.ones((1, filled), F32)
    for h in range(1, classes):
        scales = jnp.where(lane >= h * bases, 1.0 / (2 * h + 1), scales)
    line = lax.broadcasted_iota(jnp.int32, order_ref.shape, 0)
    lane = lax.broadcasted_iota(jnp.int32, order_ref.shape, 1)
    whose = jnp.zeros(order_ref.shape, jnp.int32)
    for q in range(1, classes * groups):
        whose = whose + (line >= q * unit).astype(jnp.int32)
    inside = line - whose * unit
    goal = whose * own + inside + jnp.where(inside >= own, filled - own, 0)
    order_ref[...] = jnp.where((lane == goal) & (inside < 2 * own), 1.0, 0.0).astype(BF16)

    @pl.when(has_low)
    def _():
        halo_up().wait_recv()

    @pl.when(jnp.logical_not(has_low))
    def _():
        halo[0] = jnp.zeros(halo.shape[1:], BF16)

    @pl.when(has_high)
    def _():
        halo_down().wait_recv()

    @pl.when(jnp.logical_not(has_high))
    def _():
        halo[1] = jnp.zeros(halo.shape[1:], BF16)

    @pl.loop(0, dates // 16)
    def _(g):
        taps = taps_of(g)
        for part in range(2):
            at, row = fir_rows(part, g)
            low = [halo[0, q, at, :].astype(F32) for q in range(reach)]
            low += [row(q) for q in range(2 * reach)]
            high = [row(rows - 2 * reach + q) for q in range(2 * reach)]
            high += [halo[1, q, at, :].astype(F32) for q in range(reach)]
            for i in range(reach):
                fir(i, at, taps, low[i : i + taps_count])
                fir(rows - reach + i, at, taps, high[i : i + taps_count])

    def w_copy(o, src):
        return remote(
            wsend.at[peers[o]],
            what.at[:, pl.ds(pl.multiple_of(src * dates, dates), dates), :],
            s_w.at[o], r_w.at[src], peers[o], az,
        )

    for o in list(range(1, groups)) + [0]:
        b = peers[o]
        if o:
            idx_copy(o, b).wait_recv()
        chosen = idx_all[b][0:1, :]
        pixel = lax.broadcasted_iota(jnp.int32, (block_rows * cols, 2 * looks), 0)
        pick = (pixel == chosen).astype(F32).astype(BF16)
        sample = jnp.dot(z[b], pick, preferred_element_type=F32)
        left = lax.broadcasted_iota(jnp.int32, (dates, 2 * looks), 1) < looks
        real, imag = sample[:dates], sample[dates:]
        top = jnp.where(left, real, -imag).astype(BF16)
        bottom = jnp.where(left, imag, real).astype(BF16)
        if o:
            wsend[b, 0] = top
            wsend[b, 1] = bottom
            w_copy(o, me).start()
        else:
            own = pl.ds(pl.multiple_of(me * dates, dates), dates)
            what[0, own, :] = top
            what[1, own, :] = bottom
    for o in range(1, groups):
        w_copy(o, peers[o]).wait_recv()

    whole = what[...].reshape(2 * groups * dates, 2 * looks)
    real, imag = project_gain(
        whole, level_ref[...].astype(F32) / 16.0, masked_ref[...], turned_ref[...], scales, looks
    )
    vsend[0] = real
    vsend[1] = imag

    def v_copy(o, src):
        return remote(
            vsend.at[:, pl.ds(pl.multiple_of(peers[o] * dates, dates), dates), :],
            vrecv.at[src], s_v.at[o], r_v.at[src], peers[o], az,
        )

    for o in range(1, groups):
        v_copy(o, me).start()
    vrecv[me] = vsend[:, pl.ds(pl.multiple_of(me * dates, dates), dates), :]

    for o in range(groups):
        b = peers[o]
        if o:
            v_copy(o, b).wait_recv()
        v_re = vrecv[b, 0]
        v_im = vrecv[b, 1]
        upper = jnp.concatenate([v_re, v_im], axis=0)
        lower = jnp.concatenate([-v_im, v_re], axis=0)
        mix = lax.dot_general(
            order_ref[...], jnp.concatenate([upper, lower], axis=1),
            (((1,), (1,)), ((), ())), preferred_element_type=F32,
        ).astype(BF16)
        found = jnp.dot(mix, z[b], preferred_element_type=F32)
        for i in range(block_rows):
            u[SMOOTH_REACH + b * block_rows + i] = found[:, i * cols : (i + 1) * cols]

    def smooth(r, d, place):
        total = None
        for h in range(classes):
            at = pl.ds(pl.multiple_of((h * groups + d) * unit, 8), unit)
            for j in range(-h, h + 1):
                if 0 <= place + j < rows:
                    term = u[r + j + SMOOTH_REACH, at, :]
                    total = term if total is None else total + term
        return total

    def e_copy(side, o, src, target):
        return remote(
            esend.at[side, peers[o]], erecv.at[1 - side, src],
            s_e.at[side, o], r_e.at[1 - side, src], peers[o], target,
        )

    for o in range(groups):
        d = peers[o]
        for i in range(SMOOTH_REACH):
            esend[0, d, i] = smooth(i - SMOOTH_REACH, d, i - SMOOTH_REACH).astype(BF16)
            esend[1, d, i] = smooth(rows + i, d, rows + i).astype(BF16)
        pl.when(has_low)(lambda o=o: e_copy(0, o, me, az - 1).start())
        pl.when(has_high)(lambda o=o: e_copy(1, o, me, az + 1).start())

    def p_copy(o, src):
        return remote(psend.at[peers[o]], precv.at[src], s_p.at[o], r_p.at[src], peers[o], az)

    def smooth_block(b, d, put):
        first = b * block_rows
        sums = [None] * block_rows
        for h in range(classes):
            at = pl.ds(pl.multiple_of((h * groups + d) * unit, 8), unit)
            terms = [u[first + SMOOTH_REACH + j, at, :] for j in range(-h, block_rows + h)]
            for i in range(block_rows):
                for term in terms[i : i + 2 * h + 1]:
                    sums[i] = term if sums[i] is None else sums[i] + term
        for i in range(block_rows):
            put(first + i, sums[i])

    for o in range(1, groups):
        d = peers[o]

        def put_sent(r, row, d=d):
            psend[d, r] = row.astype(BF16)

        @pl.loop(0, groups)
        def _(b):
            smooth_block(b, d, put_sent)

        p_copy(o, me).start()

    def put_own(r, row):
        out_ref[r] = row

    @pl.loop(0, groups)
    def _(b):
        smooth_block(b, me, put_own)

    @pl.when(has_low)
    def _():
        for o in range(groups):
            e_copy(1, o, peers[o], az - 1).wait_recv()
        for i in range(SMOOTH_REACH):
            for o in range(groups):
                out_ref[i] += erecv[0, peers[o], i].astype(F32)

    @pl.when(has_high)
    def _():
        for o in range(groups):
            e_copy(0, o, peers[o], az + 1).wait_recv()
        for i in range(SMOOTH_REACH):
            for o in range(groups):
                out_ref[rows - SMOOTH_REACH + i] += erecv[1, peers[o], i].astype(F32)

    for o in range(1, groups):
        p_copy(o, peers[o]).wait_recv()
        out_ref[...] += precv[peers[o]].astype(F32)

    pl.when(has_low)(lambda: halo_down().wait_send())
    pl.when(has_high)(lambda: halo_up().wait_send())
    for o in range(groups):
        if o:
            idx_copy(o, me).wait_send()
            w_copy(o, me).wait_send()
            v_copy(o, me).wait_send()
            p_copy(o, me).wait_send()
        pl.when(has_low)(lambda o=o: e_copy(0, o, me, az - 1).wait_send())
        pl.when(has_high)(lambda o=o: e_copy(1, o, me, az + 1).wait_send())


def on_device(slc_stack, fir_taps, look_index, shrink_level, window_half, basis):
    parts, dates, rows, cols = slc_stack.shape
    groups = lax.axis_size("date")
    slabs = lax.axis_size("az")
    taps_count = fir_taps.shape[1]
    looks = look_index.shape[2]
    bases, all_dates = basis.shape
    own = bases // groups
    unit = -(-2 * own // 8) * 8
    classes = SMOOTH_REACH + 1

    pitch = rows + 8
    filled = -(-classes * bases // 128) * 128

    block_rows = rows // groups
    dma = pltpu.SemaphoreType.DMA
    vmem = pl.BlockSpec(memory_space=pltpu.VMEM)
    scratch = [
        pltpu.VMEM((2 * dates * pitch, cols), F32),
        pltpu.VMEM((2, taps_count // 2, 2 * dates, cols), BF16),
        pltpu.VMEM((2, taps_count // 2, 2 * dates, cols), BF16),
        pltpu.VMEM((8, 2 * looks), jnp.int32),
        pltpu.VMEM((groups, 8, 2 * looks), jnp.int32),
        pltpu.VMEM((filled, all_dates), BF16),
        pltpu.VMEM((all_dates, filled), F32),
        pltpu.VMEM((classes * groups * unit, 2 * filled), BF16),
        pltpu.VMEM((groups, 2 * dates, block_rows * cols), BF16),
        pltpu.VMEM((groups, 2, dates, 2 * looks), BF16),
        pltpu.VMEM((2, all_dates, 2 * looks), BF16),
        pltpu.VMEM((2, all_dates, filled), BF16),
        pltpu.VMEM((groups, 2, dates, filled), BF16),
        pltpu.VMEM((rows + 2 * SMOOTH_REACH, classes * groups * unit, cols), F32),
        pltpu.VMEM((groups, rows, unit, cols), BF16),
        pltpu.VMEM((groups, rows, unit, cols), BF16),
        pltpu.VMEM((2, groups, SMOOTH_REACH, unit, cols), BF16),
        pltpu.VMEM((2, groups, SMOOTH_REACH, unit, cols), BF16),
        dma((2,)), dma((2,)),
        dma((groups,)), dma((groups,)),
        dma((groups,)), dma((groups,)),
        dma((groups,)), dma((groups,)),
        dma((groups,)), dma((groups,)),
        dma((2, groups)), dma((2, groups)),
    ]
    out = pl.pallas_call(
        functools.partial(kernel, groups, slabs, unit, own, pitch, filled),
        out_shape=jax.ShapeDtypeStruct((rows, unit, cols), F32),
        in_specs=[vmem] * 6,
        out_specs=vmem,
        scratch_shapes=scratch,
        compiler_params=pltpu.CompilerParams(
            collective_id=0, has_side_effects=True, vmem_limit_bytes=60 * 2**20
        ),
    )(
        slc_stack, fir_taps, look_index.reshape(1, looks), shrink_level,
        window_half.reshape(1, all_dates), basis,
    )
    out = out[:, : 2 * own].reshape(rows, 2, own, cols)
    return out.transpose(2, 1, 0, 3)


def solution(mesh):
    in_specs = (
        P(None, "date", "az", None),
        P("date", None),
        P("az", "date", None),
        P("az", "date"),
        P(),
        P(),
    )
    out_specs = P("date", None, "az", None)
    return jax.shard_map(
        on_device, mesh=mesh, in_specs=in_specs, out_specs=out_specs, check_vma=False
    )
```

```python
import functools

import jax
import jax.numpy as jnp
from jax import lax
from jax.experimental import pallas as pl
from jax.experimental.pallas import tpu as pltpu
from jax.sharding import PartitionSpec as P

NS_ITERS = 6
SMOOTH_REACH = 2
MESH = pl.DeviceIdType.MESH
HIGHEST = lax.Precision.HIGHEST
F32 = jnp.float32
BF16 = jnp.bfloat16


def three_terms(array):
    high = array.astype(BF16)
    rest = array - high.astype(F32)
    middle = rest.astype(BF16)
    low = (rest - middle.astype(F32)).astype(BF16)
    return high, middle, low


def exact_dot(left, right):
    l0, l1, l2 = three_terms(left)
    r0, r1, r2 = three_terms(right)
    width = right.shape[1]
    small = jnp.dot(
        jnp.concatenate([l0, l1], axis=1),
        jnp.concatenate(
            [jnp.concatenate([r1, r2], axis=1), jnp.concatenate([r0, r1], axis=1)], axis=0
        ),
        preferred_element_type=F32,
    )
    large = jnp.dot(
        jnp.concatenate([l0, l2], axis=1), jnp.concatenate([r0, r0], axis=0),
        preferred_element_type=F32,
    )
    return large + (small[:, :width] + small[:, width:])


def split_dot(left, right):
    high = left.astype(BF16)
    low = (left - high.astype(F32)).astype(BF16)
    both = lax.dot_general(
        jnp.concatenate([high, low], axis=0), right, (((1,), (1,)), ((), ())),
        preferred_element_type=F32,
    )
    return both[: left.shape[0]] + both[left.shape[0] :]


def project_gain(top, what, weight, masked, spread, scales, looks):
    dates2, width = what.shape
    dates = dates2 // 2
    gram = lax.dot_general(what, what, (((0,), (0,)), ((), ())), preferred_element_type=F32)
    line = lax.broadcasted_iota(jnp.int32, (width, width), 0)
    column = lax.broadcasted_iota(jnp.int32, (width, width), 1)
    eye = (line == column).astype(F32)
    left = lax.broadcasted_iota(jnp.int32, (looks, width), 1) < looks

    def total(array):
        return jnp.sum(jnp.sum(array, axis=1, keepdims=True), axis=0, keepdims=True)

    def full(top):
        turn = pltpu.roll(top, looks, 1)
        return jnp.concatenate([top, jnp.where(left, -turn, turn)], axis=0)

    trace = total(gram * eye) * 0.5
    norm = total(gram * gram) * 0.5
    mu = trace / (looks * dates) + 1e-06
    alpha = (1.0 - weight) / looks
    c = (1.0 + weight) * mu
    core = alpha * gram
    square = alpha * alpha * norm + 2.0 * c * alpha * trace + c * c * dates
    scale = 1.0 / jnp.sqrt(square)
    rho = 1.0 - scale * c
    whole = rho * eye - scale * core
    eye = eye[:looks]
    r = whole[:looks]
    dr = -scale * (rho * eye + r)
    df = -scale * eye
    f0 = 1.0 + rho
    r = exact_dot(r, whole)
    rho = rho * rho
    for step in range(1, NS_ITERS):
        whole = full(r)
        if step == NS_ITERS - 1:
            df = f0 * dr + df + exact_dot(df, whole)
            f0 = f0 * (1.0 + rho)
        elif step == 1:
            out = exact_dot(jnp.concatenate([dr, r], axis=0), whole)
            df = f0 * dr + df - scale * r
            f0 = f0 * (1.0 + rho)
            dr = rho * dr + out[:looks]
            r = out[looks:]
            rho = rho * rho
        else:
            out = exact_dot(jnp.concatenate([df, dr, r], axis=0), whole)
            df = f0 * dr + df + out[:looks]
            f0 = f0 * (1.0 + rho)
            dr = rho * dr + out[looks : 2 * looks]
            r = out[2 * looks :]
            rho = rho * rho
    inner = full(scale * (f0 * eye + weight * mu * df + exact_dot(df, core)))
    base = weight * mu * scale * f0
    seen = jnp.dot(masked, top, preferred_element_type=F32)
    small = exact_dot(alpha * seen, inner)
    return (split_dot(small, what) + base * spread) * scales


def kernel(
    groups, slabs, unit, own, pitch,
    x_ref, taps_ref, look_ref, level_ref, window_ref, basis_ref, out_ref,
    xf, halo_send, halo, idx_send, idx_all, masked_ref, spread_ref, order_ref,
    z, wsend, what, vsend, vrecv, u, mine, psend, precv, esend, erecv,
    s_halo, r_halo, s_idx, r_idx, s_w, r_w, s_v, r_v, s_p, r_p, s_e, r_e,
):
    me = lax.axis_index("date")
    az = lax.axis_index("az")
    _, dates, rows, cols = x_ref.shape
    taps_count = taps_ref.shape[1]
    looks = look_ref.shape[1]
    bases = basis_ref.shape[0]
    block_rows = rows // groups
    reach = taps_count // 2
    classes = SMOOTH_REACH + 1
    has_low = az > 0
    has_high = az < slabs - 1

    barrier = pltpu.get_barrier_semaphore()
    peers = [lax.rem(me + o, groups) for o in range(groups)]

    def greet(d, a):
        pl.semaphore_signal(barrier, inc=1, device_id={"date": d, "az": a}, device_id_type=MESH)

    for o in range(1, groups):
        greet(peers[o], az)

    @pl.when(has_low)
    def _():
        for o in range(groups):
            greet(peers[o], az - 1)

    @pl.when(has_high)
    def _():
        for o in range(groups):
            greet(peers[o], az + 1)

    chosen = jnp.broadcast_to(look_ref[...], (8, looks))
    idx_send[...] = jnp.concatenate([chosen, chosen], axis=1)

    def widen(t):
        for part in range(2):
            at = pl.ds(pl.multiple_of((part * dates + t) * pitch, 8), rows)
            xf[at, :] = x_ref[part, t].astype(F32)

    @pl.loop(0, dates // 8)
    def _(g):
        for t in range(8):
            widen(g * 8 + t)

    def fir_rows(part, g):
        first = part * dates + g * 16
        return (
            pl.ds(pl.multiple_of(first, 16), 16),
            lambda r: xf[pl.ds(first * pitch + r, 16, stride=pitch), :],
        )

    @pl.loop(0, dates // 16)
    def _(g):
        for part in range(2):
            at, row = fir_rows(part, g)
            for q in range(reach):
                halo_send[0, q, at, :] = row(q).astype(BF16)
                halo_send[1, q, at, :] = row(rows - reach + q).astype(BF16)

    pl.semaphore_wait(
        barrier,
        groups - 1 + groups * (has_low.astype(jnp.int32) + has_high.astype(jnp.int32)),
    )

    def remote(src, dst, send, recv, d, a):
        return pltpu.make_async_remote_copy(
            src_ref=src, dst_ref=dst, send_sem=send, recv_sem=recv,
            device_id={"date": d, "az": a}, device_id_type=MESH,
        )

    def halo_down():
        return remote(halo_send.at[0], halo.at[1], s_halo.at[0], r_halo.at[1], me, az - 1)

    def halo_up():
        return remote(halo_send.at[1], halo.at[0], s_halo.at[1], r_halo.at[0], me, az + 1)

    def idx_copy(o, src):
        return remote(idx_send, idx_all.at[src], s_idx.at[o], r_idx.at[src], peers[o], az)

    pl.when(has_low)(lambda: halo_down().start())
    pl.when(has_high)(lambda: halo_up().start())
    for o in range(1, groups):
        idx_copy(o, me).start()
    idx_all[me] = idx_send[...]

    def taps_of(g):
        taps = taps_ref[pl.ds(pl.multiple_of(g * 16, 16), 16), :]
        return [jnp.broadcast_to(taps[:, j : j + 1], (16, cols)) for j in range(taps_count)]

    def fir(r, at, taps, window):
        total = taps[0] * window[0]
        for j in range(1, taps_count):
            total = total + taps[j] * window[j]
        b, i = r // block_rows, r % block_rows
        z[b, at, i * cols : (i + 1) * cols] = total.astype(BF16)

    @pl.loop(0, dates // 16)
    def _(g):
        taps = taps_of(g)
        for part in range(2):
            at, row = fir_rows(part, g)
            window = [row(r) for r in range(2 * reach)]
            for r in range(reach, rows - reach):
                window = window[-2 * reach :] + [row(r + reach)]
                fir(r, at, taps, window)

    zeros = jnp.zeros((SMOOTH_REACH,) + u.shape[1:], F32)
    u[0:SMOOTH_REACH] = zeros
    u[rows + SMOOTH_REACH : rows + 2 * SMOOTH_REACH] = zeros
    basis = basis_ref[...].astype(F32)
    masked = [jnp.where(window_ref[...] == h, basis, 0.0) for h in range(classes)]
    masked = jnp.concatenate(masked, axis=0)
    masked_ref[...] = masked.astype(BF16)
    spread = []
    for d in range(groups):
        part = masked[:, d * dates : (d + 1) * dates]
        spread += [part, jnp.zeros_like(part)]
    spread_ref[...] = jnp.concatenate(spread, axis=1)
    line = lax.broadcasted_iota(jnp.int32, (classes * bases, 1), 0)
    scales = jnp.ones((classes * bases, 1), F32)
    for h in range(1, classes):
        scales = jnp.where(line >= h * bases, 1.0 / (2 * h + 1), scales)
    line = lax.broadcasted_iota(jnp.int32, order_ref.shape, 0)
    lane = lax.broadcasted_iota(jnp.int32, order_ref.shape, 1)
    whose = jnp.zeros(order_ref.shape, jnp.int32)
    for q in range(1, classes * groups):
        whose = whose + (line >= q * unit).astype(jnp.int32)
    inside = line - whose * unit
    goal = whose * own + (inside >> 1) + (inside & 1) * (classes * bases)
    order_ref[...] = jnp.where((lane == goal) & (inside < 2 * own), 1.0, 0.0).astype(BF16)

    @pl.when(has_low)
    def _():
        halo_up().wait_recv()

    @pl.when(jnp.logical_not(has_low))
    def _():
        halo[0] = jnp.zeros(halo.shape[1:], BF16)

    @pl.when(has_high)
    def _():
        halo_down().wait_recv()

    @pl.when(jnp.logical_not(has_high))
    def _():
        halo[1] = jnp.zeros(halo.shape[1:], BF16)

    @pl.loop(0, dates // 16)
    def _(g):
        taps = taps_of(g)
        for part in range(2):
            at, row = fir_rows(part, g)
            low = [halo[0, q, at, :].astype(F32) for q in range(reach)]
            low += [row(q) for q in range(2 * reach)]
            high = [row(rows - 2 * reach + q) for q in range(2 * reach)]
            high += [halo[1, q, at, :].astype(F32) for q in range(reach)]
            for i in range(reach):
                fir(i, at, taps, low[i : i + taps_count])
                fir(rows - reach + i, at, taps, high[i : i + taps_count])

    def w_copy(o, src):
        return remote(
            wsend.at[peers[o]], what.at[src],
            s_w.at[o], r_w.at[src], peers[o], az,
        )

    for o in list(range(1, groups)) + [0]:
        b = peers[o]
        if o:
            idx_copy(o, b).wait_recv()
        chosen = idx_all[b][0:1, :]
        pixel = lax.broadcasted_iota(jnp.int32, (block_rows * cols, 2 * looks), 0)
        pick = (pixel == chosen).astype(F32).astype(BF16)
        sample = jnp.dot(z[b], pick, preferred_element_type=F32)
        left = lax.broadcasted_iota(jnp.int32, (dates, 2 * looks), 1) < looks
        sample = jnp.where(left, sample[:dates], sample[dates:]).astype(BF16)
        if o:
            wsend[b] = sample
            w_copy(o, me).start()
        else:
            what[me] = sample
    for o in range(1, groups):
        w_copy(o, peers[o]).wait_recv()

    tops = []
    both = []
    for d in range(groups):
        sample = what[d].astype(F32)
        top = jnp.where(left, sample, -sample).astype(BF16)
        tops.append(top)
        both += [top, pltpu.roll(sample, looks, 1).astype(BF16)]
    found = project_gain(
        jnp.concatenate(tops, axis=0), jnp.concatenate(both, axis=0),
        level_ref[...].astype(F32) / 16.0, masked_ref[...], spread_ref[...], scales, looks,
    ).astype(BF16)
    for d in range(groups):
        vsend[d] = found[:, d * 2 * dates : (d + 1) * 2 * dates]

    def v_copy(o, src):
        return remote(vsend.at[peers[o]], vrecv.at[src], s_v.at[o], r_v.at[src], peers[o], az)

    for o in range(1, groups):
        v_copy(o, me).start()
    vrecv[me] = vsend[me]

    for o in range(groups):
        b = peers[o]
        if o:
            v_copy(o, b).wait_recv()
        upper = vrecv[b]
        lower = jnp.concatenate([-upper[:, dates:], upper[:, :dates]], axis=1)
        mix = jnp.dot(
            order_ref[...], jnp.concatenate([upper, lower], axis=0), preferred_element_type=F32
        ).astype(BF16)
        found = jnp.dot(mix, z[b], preferred_element_type=F32)
        for i in range(block_rows):
            u[SMOOTH_REACH + b * block_rows + i] = found[:, i * cols : (i + 1) * cols]

    def smooth(r, d, place):
        total = None
        for h in range(classes):
            at = pl.ds(pl.multiple_of((h * groups + d) * unit, 8), unit)
            for j in range(-h, h + 1):
                if 0 <= place + j < rows:
                    term = u[r + j + SMOOTH_REACH, at, :]
                    total = term if total is None else total + term
        return total

    def e_copy(side, o, src, target):
        return remote(
            esend.at[side, peers[o]], erecv.at[1 - side, src],
            s_e.at[side, o], r_e.at[1 - side, src], peers[o], target,
        )

    for o in range(groups):
        d = peers[o]
        for i in range(SMOOTH_REACH):
            esend[0, d, i] = smooth(i - SMOOTH_REACH, d, i - SMOOTH_REACH).astype(BF16)
            esend[1, d, i] = smooth(rows + i, d, rows + i).astype(BF16)
        pl.when(has_low)(lambda o=o: e_copy(0, o, me, az - 1).start())
        pl.when(has_high)(lambda o=o: e_copy(1, o, me, az + 1).start())

    def p_copy(o, src):
        return remote(psend.at[peers[o]], precv.at[src], s_p.at[o], r_p.at[src], peers[o], az)

    def smooth_block(b, d, put):
        first = b * block_rows
        sums = [None] * block_rows
        for h in range(classes):
            at = pl.ds(pl.multiple_of((h * groups + d) * unit, 8), unit)
            terms = [u[first + SMOOTH_REACH + j, at, :] for j in range(-h, block_rows + h)]
            for i in range(block_rows):
                for term in terms[i : i + 2 * h + 1]:
                    sums[i] = term if sums[i] is None else sums[i] + term
        for i in range(block_rows):
            put(first + i, sums[i])

    for o in range(1, groups):
        d = peers[o]

        def put_sent(r, row, d=d):
            psend[d, r] = row.astype(BF16)

        @pl.loop(0, groups)
        def _(b):
            smooth_block(b, d, put_sent)

        p_copy(o, me).start()

    def put_own(r, row):
        mine[r] = row

    @pl.loop(0, groups)
    def _(b):
        smooth_block(b, me, put_own)

    @pl.when(has_low)
    def _():
        for o in range(groups):
            e_copy(1, o, peers[o], az - 1).wait_recv()
        for i in range(SMOOTH_REACH):
            for o in range(groups):
                mine[i] += erecv[0, peers[o], i].astype(F32)

    @pl.when(has_high)
    def _():
        for o in range(groups):
            e_copy(0, o, peers[o], az + 1).wait_recv()
        for i in range(SMOOTH_REACH):
            for o in range(groups):
                mine[rows - SMOOTH_REACH + i] += erecv[1, peers[o], i].astype(F32)

    for o in range(1, groups):
        p_copy(o, peers[o]).wait_recv()
        if o < groups - 1:
            mine[...] += precv[peers[o]].astype(F32)

    @pl.loop(0, groups)
    def _(b):
        for i in range(block_rows):
            r = b * block_rows + i
            row = mine[r] + precv[peers[groups - 1], r].astype(F32)
            out_ref[pl.ds(r, 2 * own, stride=rows), :] = row[: 2 * own]

    pl.when(has_low)(lambda: halo_down().wait_send())
    pl.when(has_high)(lambda: halo_up().wait_send())
    for o in range(groups):
        if o:
            idx_copy(o, me).wait_send()
            w_copy(o, me).wait_send()
            v_copy(o, me).wait_send()
            p_copy(o, me).wait_send()
        pl.when(has_low)(lambda o=o: e_copy(0, o, me, az - 1).wait_send())
        pl.when(has_high)(lambda o=o: e_copy(1, o, me, az + 1).wait_send())


def on_device(slc_stack, fir_taps, look_index, shrink_level, window_half, basis):
    parts, dates, rows, cols = slc_stack.shape
    groups = lax.axis_size("date")
    slabs = lax.axis_size("az")
    taps_count = fir_taps.shape[1]
    looks = look_index.shape[2]
    bases, all_dates = basis.shape
    own = bases // groups
    unit = -(-2 * own // 8) * 8
    classes = SMOOTH_REACH + 1

    pitch = rows + 8

    block_rows = rows // groups
    dma = pltpu.SemaphoreType.DMA
    vmem = pl.BlockSpec(memory_space=pltpu.VMEM)
    scratch = [
        pltpu.VMEM((2 * dates * pitch, cols), F32),
        pltpu.VMEM((2, taps_count // 2, 2 * dates, cols), BF16),
        pltpu.VMEM((2, taps_count // 2, 2 * dates, cols), BF16),
        pltpu.VMEM((8, 2 * looks), jnp.int32),
        pltpu.VMEM((groups, 8, 2 * looks), jnp.int32),
        pltpu.VMEM((classes * bases, all_dates), BF16),
        pltpu.VMEM((classes * bases, 2 * all_dates), F32),
        pltpu.VMEM((classes * groups * unit, 2 * classes * bases), BF16),
        pltpu.VMEM((groups, 2 * dates, block_rows * cols), BF16),
        pltpu.VMEM((groups, dates, 2 * looks), BF16),
        pltpu.VMEM((groups, dates, 2 * looks), BF16),
        pltpu.VMEM((groups, classes * bases, 2 * dates), BF16),
        pltpu.VMEM((groups, classes * bases, 2 * dates), BF16),
        pltpu.VMEM((rows + 2 * SMOOTH_REACH, classes * groups * unit, cols), F32),
        pltpu.VMEM((rows, unit, cols), F32),
        pltpu.VMEM((groups, rows, unit, cols), BF16),
        pltpu.VMEM((groups, rows, unit, cols), BF16),
        pltpu.VMEM((2, groups, SMOOTH_REACH, unit, cols), BF16),
        pltpu.VMEM((2, groups, SMOOTH_REACH, unit, cols), BF16),
        dma((2,)), dma((2,)),
        dma((groups,)), dma((groups,)),
        dma((groups,)), dma((groups,)),
        dma((groups,)), dma((groups,)),
        dma((groups,)), dma((groups,)),
        dma((2, groups)), dma((2, groups)),
    ]
    out = pl.pallas_call(
        functools.partial(kernel, groups, slabs, unit, own, pitch),
        out_shape=jax.ShapeDtypeStruct((2 * own * rows, cols), F32),
        in_specs=[vmem] * 6,
        out_specs=vmem,
        scratch_shapes=scratch,
        compiler_params=pltpu.CompilerParams(
            collective_id=0, has_side_effects=True, vmem_limit_bytes=60 * 2**20
        ),
    )(
        slc_stack, fir_taps, look_index.reshape(1, looks), shrink_level,
        window_half.reshape(1, all_dates), basis,
    )
    return out.reshape(own, 2, rows, cols)


def solution(mesh):
    in_specs = (
        P(None, "date", "az", None),
        P("date", None),
        P("az", "date", None),
        P("az", "date"),
        P(),
        P(),
    )
    out_specs = P("date", None, "az", None)
    return jax.shard_map(
        on_device, mesh=mesh, in_specs=in_specs, out_specs=out_specs, check_vma=False
    )
```

```python
import functools

import jax
import jax.numpy as jnp
from jax import lax
from jax.experimental import pallas as pl
from jax.experimental.pallas import tpu as pltpu
from jax.sharding import PartitionSpec as P

NS_ITERS = 6
SMOOTH_REACH = 2
MESH = pl.DeviceIdType.MESH
HIGHEST = lax.Precision.HIGHEST
F32 = jnp.float32
BF16 = jnp.bfloat16


def three_terms(array):
    high = array.astype(BF16)
    rest = array - high.astype(F32)
    middle = rest.astype(BF16)
    low = (rest - middle.astype(F32)).astype(BF16)
    return high, middle, low


def exact_dot(left, right):
    l0, l1, l2 = three_terms(left)
    r0, r1, r2 = three_terms(right)
    width = right.shape[1]
    small = jnp.dot(
        jnp.concatenate([l0, l1], axis=1),
        jnp.concatenate(
            [jnp.concatenate([r1, r2], axis=1), jnp.concatenate([r0, r1], axis=1)], axis=0
        ),
        preferred_element_type=F32,
    )
    large = jnp.dot(
        jnp.concatenate([l0, l2], axis=1), jnp.concatenate([r0, r0], axis=0),
        preferred_element_type=F32,
    )
    return large + (small[:, :width] + small[:, width:])


def split_dot(left, right):
    high = left.astype(BF16)
    low = (left - high.astype(F32)).astype(BF16)
    both = lax.dot_general(
        jnp.concatenate([high, low], axis=0), right, (((1,), (1,)), ((), ())),
        preferred_element_type=F32,
    )
    return both[: left.shape[0]] + both[left.shape[0] :]


def project_gain(top, what, weight, masked, spread, scales, looks):
    dates2, width = what.shape
    dates = dates2 // 2
    gram = lax.dot_general(what, what, (((0,), (0,)), ((), ())), preferred_element_type=F32)
    line = lax.broadcasted_iota(jnp.int32, (width, width), 0)
    column = lax.broadcasted_iota(jnp.int32, (width, width), 1)
    eye = (line == column).astype(F32)
    left = lax.broadcasted_iota(jnp.int32, (looks, width), 1) < looks

    def total(array):
        return jnp.sum(jnp.sum(array, axis=1, keepdims=True), axis=0, keepdims=True)

    def full(top):
        turn = pltpu.roll(top, looks, 1)
        return jnp.concatenate([top, jnp.where(left, -turn, turn)], axis=0)

    trace = total(gram * eye) * 0.5
    norm = total(gram * gram) * 0.5
    mu = trace / (looks * dates) + 1e-06
    alpha = (1.0 - weight) / looks
    c = (1.0 + weight) * mu
    core = alpha * gram
    square = alpha * alpha * norm + 2.0 * c * alpha * trace + c * c * dates
    scale = 1.0 / jnp.sqrt(square)
    rho = 1.0 - scale * c
    whole = rho * eye - scale * core
    eye = eye[:looks]
    r = whole[:looks]
    dr = -scale * (rho * eye + r)
    df = -scale * eye
    f0 = 1.0 + rho
    r = exact_dot(r, whole)
    rho = rho * rho
    for step in range(1, NS_ITERS):
        whole = full(r)
        if step == NS_ITERS - 1:
            df = f0 * dr + df + exact_dot(df, whole)
            f0 = f0 * (1.0 + rho)
        elif step == 1:
            out = exact_dot(jnp.concatenate([dr, r], axis=0), whole)
            df = f0 * dr + df - scale * r
            f0 = f0 * (1.0 + rho)
            dr = rho * dr + out[:looks]
            r = out[looks:]
            rho = rho * rho
        else:
            out = exact_dot(jnp.concatenate([df, dr, r], axis=0), whole)
            df = f0 * dr + df + out[:looks]
            f0 = f0 * (1.0 + rho)
            dr = rho * dr + out[looks : 2 * looks]
            r = out[2 * looks :]
            rho = rho * rho
    inner = full(scale * (f0 * eye + weight * mu * df + exact_dot(df, core)))
    base = weight * mu * scale * f0
    seen = jnp.dot(masked, top, preferred_element_type=F32)
    small = exact_dot(alpha * seen, inner)
    return (split_dot(small, what) + base * spread) * scales


def kernel(
    groups, slabs, unit, own, pitch,
    x_ref, taps_ref, look_ref, level_ref, window_ref, basis_ref, out_ref,
    xf, halo_send, halo, idx_send, idx_all, masked_ref, spread_ref, order_ref,
    z, wsend, what, vsend, vrecv, u, mine, psend, precv, esend, erecv,
    s_halo, r_halo, s_idx, r_idx, s_w, r_w, s_v, r_v, s_p, r_p, s_e, r_e,
):
    me = lax.axis_index("date")
    az = lax.axis_index("az")
    _, dates, rows, cols = x_ref.shape
    taps_count = taps_ref.shape[1]
    looks = look_ref.shape[1]
    bases = basis_ref.shape[0]
    block_rows = rows // groups
    reach = taps_count // 2
    classes = SMOOTH_REACH + 1
    has_low = az > 0
    has_high = az < slabs - 1

    barrier = pltpu.get_barrier_semaphore()
    peers = [lax.rem(me + o, groups) for o in range(groups)]

    def greet(d, a):
        pl.semaphore_signal(barrier, inc=1, device_id={"date": d, "az": a}, device_id_type=MESH)

    for o in range(1, groups):
        greet(peers[o], az)

    @pl.when(has_low)
    def _():
        for o in range(groups):
            greet(peers[o], az - 1)

    @pl.when(has_high)
    def _():
        for o in range(groups):
            greet(peers[o], az + 1)

    chosen = jnp.broadcast_to(look_ref[...], (8, looks))
    idx_send[...] = jnp.concatenate([chosen, chosen], axis=1)

    def widen(t):
        for part in range(2):
            at = pl.ds(pl.multiple_of((part * dates + t) * pitch, 8), rows)
            xf[at, :] = x_ref[part, t].astype(F32)

    @pl.loop(0, dates // 8)
    def _(g):
        for t in range(8):
            widen(g * 8 + t)

    def fir_rows(part, g):
        first = part * dates + g * 16
        return (
            pl.ds(pl.multiple_of(first, 16), 16),
            lambda r: xf[pl.ds(first * pitch + r, 16, stride=pitch), :],
        )

    @pl.loop(0, dates // 16)
    def _(g):
        for part in range(2):
            at, row = fir_rows(part, g)
            for q in range(reach):
                halo_send[0, q, at, :] = row(q).astype(BF16)
                halo_send[1, q, at, :] = row(rows - reach + q).astype(BF16)

    pl.semaphore_wait(
        barrier,
        groups - 1 + groups * (has_low.astype(jnp.int32) + has_high.astype(jnp.int32)),
    )

    def remote(src, dst, send, recv, d, a):
        return pltpu.make_async_remote_copy(
            src_ref=src, dst_ref=dst, send_sem=send, recv_sem=recv,
            device_id={"date": d, "az": a}, device_id_type=MESH,
        )

    def halo_down():
        return remote(halo_send.at[0], halo.at[1], s_halo.at[0], r_halo.at[1], me, az - 1)

    def halo_up():
        return remote(halo_send.at[1], halo.at[0], s_halo.at[1], r_halo.at[0], me, az + 1)

    def idx_copy(o, src):
        return remote(idx_send, idx_all.at[src], s_idx.at[o], r_idx.at[src], peers[o], az)

    pl.when(has_low)(lambda: halo_down().start())
    pl.when(has_high)(lambda: halo_up().start())
    for o in range(1, groups):
        idx_copy(o, me).start()
    idx_all[me] = idx_send[...]

    def taps_of(g):
        taps = taps_ref[pl.ds(pl.multiple_of(g * 16, 16), 16), :]
        return [jnp.broadcast_to(taps[:, j : j + 1], (16, cols)) for j in range(taps_count)]

    def fir(r, at, taps, window):
        total = taps[0] * window[0]
        for j in range(1, taps_count):
            total = total + taps[j] * window[j]
        b, i = r // block_rows, r % block_rows
        z[b, at, i * cols : (i + 1) * cols] = total.astype(BF16)

    @pl.loop(0, dates // 16)
    def _(g):
        taps = taps_of(g)
        for part in range(2):
            at, row = fir_rows(part, g)
            window = [row(r) for r in range(2 * reach)]
            for r in range(reach, rows - reach):
                window = window[-2 * reach :] + [row(r + reach)]
                fir(r, at, taps, window)

    zeros = jnp.zeros((SMOOTH_REACH,) + u.shape[1:], F32)
    u[0:SMOOTH_REACH] = zeros
    u[rows + SMOOTH_REACH : rows + 2 * SMOOTH_REACH] = zeros
    basis = basis_ref[...].astype(F32)
    masked = [jnp.where(window_ref[...] == h, basis, 0.0) for h in range(classes)]
    masked = jnp.concatenate(masked, axis=0)
    masked_ref[...] = masked.astype(BF16)
    spread = []
    for d in range(groups):
        part = masked[:, d * dates : (d + 1) * dates]
        spread += [part, jnp.zeros_like(part)]
    spread_ref[...] = jnp.concatenate(spread, axis=1)
    line = lax.broadcasted_iota(jnp.int32, (classes * bases, 1), 0)
    scales = jnp.ones((classes * bases, 1), F32)
    for h in range(1, classes):
        scales = jnp.where(line >= h * bases, 1.0 / (2 * h + 1), scales)
    line = lax.broadcasted_iota(jnp.int32, order_ref.shape, 0)
    lane = lax.broadcasted_iota(jnp.int32, order_ref.shape, 1)
    whose = jnp.zeros(order_ref.shape, jnp.int32)
    for q in range(1, classes * groups):
        whose = whose + (line >= q * unit).astype(jnp.int32)
    inside = line - whose * unit
    goal = whose * own + (inside >> 1) + (inside & 1) * (classes * bases)
    order_ref[...] = jnp.where((lane == goal) & (inside < 2 * own), 1.0, 0.0).astype(BF16)

    @pl.when(has_low)
    def _():
        halo_up().wait_recv()

    @pl.when(jnp.logical_not(has_low))
    def _():
        halo[0] = jnp.zeros(halo.shape[1:], BF16)

    @pl.when(has_high)
    def _():
        halo_down().wait_recv()

    @pl.when(jnp.logical_not(has_high))
    def _():
        halo[1] = jnp.zeros(halo.shape[1:], BF16)

    @pl.loop(0, dates // 16)
    def _(g):
        taps = taps_of(g)
        for part in range(2):
            at, row = fir_rows(part, g)
            low = [halo[0, q, at, :].astype(F32) for q in range(reach)]
            low += [row(q) for q in range(2 * reach)]
            high = [row(rows - 2 * reach + q) for q in range(2 * reach)]
            high += [halo[1, q, at, :].astype(F32) for q in range(reach)]
            for i in range(reach):
                fir(i, at, taps, low[i : i + taps_count])
                fir(rows - reach + i, at, taps, high[i : i + taps_count])

    def w_copy(o, src):
        return remote(
            wsend.at[peers[o]], what.at[src],
            s_w.at[o], r_w.at[src], peers[o], az,
        )

    for o in list(range(1, groups)) + [0]:
        b = peers[o]
        if o:
            idx_copy(o, b).wait_recv()
        chosen = idx_all[b][0:1, :]
        pixel = lax.broadcasted_iota(jnp.int32, (block_rows * cols, 2 * looks), 0)
        pick = (pixel == chosen).astype(F32).astype(BF16)
        sample = jnp.dot(z[b], pick, preferred_element_type=F32)
        left = lax.broadcasted_iota(jnp.int32, (dates, 2 * looks), 1) < looks
        sample = jnp.where(left, sample[:dates], sample[dates:]).astype(BF16)
        if o:
            wsend[b] = sample
            w_copy(o, me).start()
        else:
            what[me] = sample
    for o in range(1, groups):
        w_copy(o, peers[o]).wait_recv()

    tops = []
    both = []
    for d in range(groups):
        sample = what[d].astype(F32)
        top = jnp.where(left, sample, -sample).astype(BF16)
        tops.append(top)
        both += [top, pltpu.roll(sample, looks, 1).astype(BF16)]
    found = project_gain(
        jnp.concatenate(tops, axis=0), jnp.concatenate(both, axis=0),
        level_ref[...].astype(F32) / 16.0, masked_ref[...], spread_ref[...], scales, looks,
    ).astype(BF16)
    for d in range(groups):
        vsend[d] = found[:, d * 2 * dates : (d + 1) * 2 * dates]

    def v_copy(o, src):
        return remote(vsend.at[peers[o]], vrecv.at[src], s_v.at[o], r_v.at[src], peers[o], az)

    for o in range(1, groups):
        v_copy(o, me).start()
    vrecv[me] = vsend[me]

    def mix_block(b):
        @pl.when(me != b)
        def _():
            v_copy(1, b).wait_recv()

        upper = vrecv[b]
        lower = jnp.concatenate([-upper[:, dates:], upper[:, :dates]], axis=1)
        mix = jnp.dot(
            order_ref[...], jnp.concatenate([upper, lower], axis=0), preferred_element_type=F32
        ).astype(BF16)
        found = jnp.dot(mix, z[b], preferred_element_type=F32)
        for i in range(block_rows):
            u[SMOOTH_REACH + b * block_rows + i] = found[:, i * cols : (i + 1) * cols]

    def smooth(r, d, place):
        total = None
        for h in range(classes):
            at = pl.ds(pl.multiple_of((h * groups + d) * unit, 8), unit)
            for j in range(-h, h + 1):
                if 0 <= place + j < rows:
                    term = u[r + j + SMOOTH_REACH, at, :]
                    total = term if total is None else total + term
        return total

    half = groups // 2
    half_rows = half * block_rows

    def p_copy(o, src, part):
        at = pl.ds(part * half_rows, half_rows)
        return remote(
            psend.at[peers[o], at], precv.at[src, at],
            s_p.at[part, o], r_p.at[part, src], peers[o], az,
        )

    def smooth_block(b, d, put):
        first = b * block_rows
        sums = [None] * block_rows
        for h in range(classes):
            at = pl.ds(pl.multiple_of((h * groups + d) * unit, 8), unit)
            terms = [u[first + SMOOTH_REACH + j, at, :] for j in range(-h, block_rows + h)]
            for i in range(block_rows):
                for term in terms[i : i + 2 * h + 1]:
                    sums[i] = term if sums[i] is None else sums[i] + term
        for i in range(block_rows):
            put(first + i, sums[i])

    for part in range(2):
        for b in range(half + 1) if part == 0 else range(half + 1, groups):
            mix_block(b)
        for o in range(1, groups):
            d = peers[o]

            def put_sent(r, row, d=d):
                psend[d, r] = row.astype(BF16)

            @pl.loop(part * half, (part + 1) * half)
            def _(b):
                smooth_block(b, d, put_sent)

            p_copy(o, me, part).start()

    def e_copy(side, o, src, target):
        return remote(
            esend.at[side, peers[o]], erecv.at[1 - side, src],
            s_e.at[side, o], r_e.at[1 - side, src], peers[o], target,
        )

    for o in range(groups):
        d = peers[o]
        for i in range(SMOOTH_REACH):
            esend[0, d, i] = smooth(i - SMOOTH_REACH, d, i - SMOOTH_REACH).astype(BF16)
            esend[1, d, i] = smooth(rows + i, d, rows + i).astype(BF16)
        pl.when(has_low)(lambda o=o: e_copy(0, o, me, az - 1).start())
        pl.when(has_high)(lambda o=o: e_copy(1, o, me, az + 1).start())

    def put_own(r, row):
        mine[r] = row

    @pl.loop(0, groups)
    def _(b):
        smooth_block(b, me, put_own)

    @pl.when(has_low)
    def _():
        for o in range(groups):
            e_copy(1, o, peers[o], az - 1).wait_recv()
        for i in range(SMOOTH_REACH):
            for o in range(groups):
                mine[i] += erecv[0, peers[o], i].astype(F32)

    @pl.when(has_high)
    def _():
        for o in range(groups):
            e_copy(0, o, peers[o], az + 1).wait_recv()
        for i in range(SMOOTH_REACH):
            for o in range(groups):
                mine[rows - SMOOTH_REACH + i] += erecv[1, peers[o], i].astype(F32)

    for o in range(1, groups):
        for part in range(2):
            p_copy(o, peers[o], part).wait_recv()
        if o < groups - 1:
            mine[...] += precv[peers[o]].astype(F32)

    @pl.loop(0, groups)
    def _(b):
        for i in range(block_rows):
            r = b * block_rows + i
            row = mine[r] + precv[peers[groups - 1], r].astype(F32)
            out_ref[pl.ds(r, 2 * own, stride=rows), :] = row[: 2 * own]

    pl.when(has_low)(lambda: halo_down().wait_send())
    pl.when(has_high)(lambda: halo_up().wait_send())
    for o in range(groups):
        if o:
            idx_copy(o, me).wait_send()
            w_copy(o, me).wait_send()
            v_copy(o, me).wait_send()
            for part in range(2):
                p_copy(o, me, part).wait_send()
        pl.when(has_low)(lambda o=o: e_copy(0, o, me, az - 1).wait_send())
        pl.when(has_high)(lambda o=o: e_copy(1, o, me, az + 1).wait_send())


def on_device(slc_stack, fir_taps, look_index, shrink_level, window_half, basis):
    parts, dates, rows, cols = slc_stack.shape
    groups = lax.axis_size("date")
    slabs = lax.axis_size("az")
    taps_count = fir_taps.shape[1]
    looks = look_index.shape[2]
    bases, all_dates = basis.shape
    own = bases // groups
    unit = -(-2 * own // 8) * 8
    classes = SMOOTH_REACH + 1

    pitch = rows + 8

    block_rows = rows // groups
    dma = pltpu.SemaphoreType.DMA
    vmem = pl.BlockSpec(memory_space=pltpu.VMEM)
    scratch = [
        pltpu.VMEM((2 * dates * pitch, cols), F32),
        pltpu.VMEM((2, taps_count // 2, 2 * dates, cols), BF16),
        pltpu.VMEM((2, taps_count // 2, 2 * dates, cols), BF16),
        pltpu.VMEM((8, 2 * looks), jnp.int32),
        pltpu.VMEM((groups, 8, 2 * looks), jnp.int32),
        pltpu.VMEM((classes * bases, all_dates), BF16),
        pltpu.VMEM((classes * bases, 2 * all_dates), F32),
        pltpu.VMEM((classes * groups * unit, 2 * classes * bases), BF16),
        pltpu.VMEM((groups, 2 * dates, block_rows * cols), BF16),
        pltpu.VMEM((groups, dates, 2 * looks), BF16),
        pltpu.VMEM((groups, dates, 2 * looks), BF16),
        pltpu.VMEM((groups, classes * bases, 2 * dates), BF16),
        pltpu.VMEM((groups, classes * bases, 2 * dates), BF16),
        pltpu.VMEM((rows + 2 * SMOOTH_REACH, classes * groups * unit, cols), F32),
        pltpu.VMEM((rows, unit, cols), F32),
        pltpu.VMEM((groups, rows, unit, cols), BF16),
        pltpu.VMEM((groups, rows, unit, cols), BF16),
        pltpu.VMEM((2, groups, SMOOTH_REACH, unit, cols), BF16),
        pltpu.VMEM((2, groups, SMOOTH_REACH, unit, cols), BF16),
        dma((2,)), dma((2,)),
        dma((groups,)), dma((groups,)),
        dma((groups,)), dma((groups,)),
        dma((groups,)), dma((groups,)),
        dma((2, groups)), dma((2, groups)),
        dma((2, groups)), dma((2, groups)),
    ]
    out = pl.pallas_call(
        functools.partial(kernel, groups, slabs, unit, own, pitch),
        out_shape=jax.ShapeDtypeStruct((2 * own * rows, cols), F32),
        in_specs=[vmem] * 6,
        out_specs=vmem,
        scratch_shapes=scratch,
        compiler_params=pltpu.CompilerParams(
            collective_id=0, has_side_effects=True, vmem_limit_bytes=60 * 2**20
        ),
    )(
        slc_stack, fir_taps, look_index.reshape(1, looks), shrink_level,
        window_half.reshape(1, all_dates), basis,
    )
    return out.reshape(own, 2, rows, cols)


def solution(mesh):
    in_specs = (
        P(None, "date", "az", None),
        P("date", None),
        P("az", "date", None),
        P("az", "date"),
        P(),
        P(),
    )
    out_specs = P("date", None, "az", None)
    return jax.shard_map(
        on_device, mesh=mesh, in_specs=in_specs, out_specs=out_specs, check_vma=False
    )
```

```python
import functools

import jax
import jax.numpy as jnp
from jax import lax
from jax.experimental import pallas as pl
from jax.experimental.pallas import tpu as pltpu
from jax.sharding import PartitionSpec as P

NS_ITERS = 6
SMOOTH_REACH = 2
MESH = pl.DeviceIdType.MESH
HIGHEST = lax.Precision.HIGHEST
F32 = jnp.float32
BF16 = jnp.bfloat16


def three_terms(array):
    high = array.astype(BF16)
    rest = array - high.astype(F32)
    middle = rest.astype(BF16)
    low = (rest - middle.astype(F32)).astype(BF16)
    return high, middle, low


def exact_dot(left, right):
    l0, l1, l2 = three_terms(left)
    r0, r1, r2 = three_terms(right)
    width = right.shape[1]
    small = jnp.dot(
        jnp.concatenate([l0, l1], axis=1),
        jnp.concatenate(
            [jnp.concatenate([r1, r2], axis=1), jnp.concatenate([r0, r1], axis=1)], axis=0
        ),
        preferred_element_type=F32,
    )
    large = jnp.dot(
        jnp.concatenate([l0, l2], axis=1), jnp.concatenate([r0, r0], axis=0),
        preferred_element_type=F32,
    )
    return large + (small[:, :width] + small[:, width:])


def split_dot(left, right):
    high = left.astype(BF16)
    low = (left - high.astype(F32)).astype(BF16)
    both = lax.dot_general(
        jnp.concatenate([high, low], axis=0), right, (((1,), (1,)), ((), ())),
        preferred_element_type=F32,
    )
    return both[: left.shape[0]] + both[left.shape[0] :]


def project_gain(top, what, weight, masked, spread, scales, looks):
    dates2, width = what.shape
    dates = dates2 // 2
    gram = lax.dot_general(what, what, (((0,), (0,)), ((), ())), preferred_element_type=F32)
    line = lax.broadcasted_iota(jnp.int32, (width, width), 0)
    column = lax.broadcasted_iota(jnp.int32, (width, width), 1)
    eye = (line == column).astype(F32)
    left = lax.broadcasted_iota(jnp.int32, (looks, width), 1) < looks

    def total(array):
        return jnp.sum(jnp.sum(array, axis=1, keepdims=True), axis=0, keepdims=True)

    def full(top):
        turn = pltpu.roll(top, looks, 1)
        return jnp.concatenate([top, jnp.where(left, -turn, turn)], axis=0)

    trace = total(gram * eye) * 0.5
    norm = total(gram * gram) * 0.5
    mu = trace / (looks * dates) + 1e-06
    alpha = (1.0 - weight) / looks
    c = (1.0 + weight) * mu
    core = alpha * gram
    square = alpha * alpha * norm + 2.0 * c * alpha * trace + c * c * dates
    scale = 1.0 / jnp.sqrt(square)
    rho = 1.0 - scale * c
    whole = rho * eye - scale * core
    eye = eye[:looks]
    r = whole[:looks]
    dr = -scale * (rho * eye + r)
    df = -scale * eye
    f0 = 1.0 + rho
    r = exact_dot(r, whole)
    rho = rho * rho
    for step in range(1, NS_ITERS):
        whole = full(r)
        if step == NS_ITERS - 1:
            df = f0 * dr + df + exact_dot(df, whole)
            f0 = f0 * (1.0 + rho)
        elif step == 1:
            out = exact_dot(jnp.concatenate([dr, r], axis=0), whole)
            df = f0 * dr + df - scale * r
            f0 = f0 * (1.0 + rho)
            dr = rho * dr + out[:looks]
            r = out[looks:]
            rho = rho * rho
        else:
            out = exact_dot(jnp.concatenate([df, dr, r], axis=0), whole)
            df = f0 * dr + df + out[:looks]
            f0 = f0 * (1.0 + rho)
            dr = rho * dr + out[looks : 2 * looks]
            r = out[2 * looks :]
            rho = rho * rho
    inner = full(scale * (f0 * eye + weight * mu * df + exact_dot(df, core)))
    base = weight * mu * scale * f0
    seen = jnp.dot(masked, top, preferred_element_type=F32)
    small = exact_dot(alpha * seen, inner)
    return (split_dot(small, what) + base * spread) * scales


def kernel(
    groups, slabs, unit, own, pitch,
    x_ref, taps_ref, look_ref, level_ref, window_ref, basis_ref, out_ref,
    xf, halo_send, halo, idx_send, idx_all, masked_ref, spread_ref, order_ref,
    z, wsend, what, vsend, vrecv, u, mine, psend, precv, esend, erecv,
    s_halo, r_halo, s_idx, r_idx, s_w, r_w, s_v, r_v, s_p, r_p, s_e, r_e,
):
    me = lax.axis_index("date")
    az = lax.axis_index("az")
    _, dates, rows, cols = x_ref.shape
    taps_count = taps_ref.shape[1]
    looks = look_ref.shape[1]
    bases = basis_ref.shape[0]
    block_rows = rows // groups
    reach = taps_count // 2
    classes = SMOOTH_REACH + 1
    has_low = az > 0
    has_high = az < slabs - 1

    barrier = pltpu.get_barrier_semaphore()
    peers = [lax.rem(me + o, groups) for o in range(groups)]

    def greet(d, a):
        pl.semaphore_signal(barrier, inc=1, device_id={"date": d, "az": a}, device_id_type=MESH)

    for o in range(1, groups):
        greet(peers[o], az)

    @pl.when(has_low)
    def _():
        greet(me, az - 1)

    @pl.when(has_high)
    def _():
        greet(me, az + 1)

    chosen = jnp.broadcast_to(look_ref[...], (8, looks))
    idx_send[...] = jnp.concatenate([chosen, chosen], axis=1)

    def widen(t):
        for part in range(2):
            at = pl.ds(pl.multiple_of((part * dates + t) * pitch, 8), rows)
            xf[at, :] = x_ref[part, t].astype(F32)

    @pl.loop(0, dates // 8)
    def _(g):
        for t in range(8):
            widen(g * 8 + t)

    def fir_rows(part, g):
        first = part * dates + g * 16
        return (
            pl.ds(pl.multiple_of(first, 16), 16),
            lambda r: xf[pl.ds(first * pitch + r, 16, stride=pitch), :],
        )

    @pl.loop(0, dates // 16)
    def _(g):
        for part in range(2):
            at, row = fir_rows(part, g)
            for q in range(reach):
                halo_send[0, q, at, :] = row(q).astype(BF16)
                halo_send[1, q, at, :] = row(rows - reach + q).astype(BF16)

    pl.semaphore_wait(
        barrier,
        groups - 1 + has_low.astype(jnp.int32) + has_high.astype(jnp.int32),
    )

    def remote(src, dst, send, recv, d, a):
        return pltpu.make_async_remote_copy(
            src_ref=src, dst_ref=dst, send_sem=send, recv_sem=recv,
            device_id={"date": d, "az": a}, device_id_type=MESH,
        )

    def halo_down():
        return remote(halo_send.at[0], halo.at[1], s_halo.at[0], r_halo.at[1], me, az - 1)

    def halo_up():
        return remote(halo_send.at[1], halo.at[0], s_halo.at[1], r_halo.at[0], me, az + 1)

    def idx_copy(o, src):
        return remote(idx_send, idx_all.at[src], s_idx.at[o], r_idx.at[src], peers[o], az)

    pl.when(has_low)(lambda: halo_down().start())
    pl.when(has_high)(lambda: halo_up().start())
    for o in range(1, groups):
        idx_copy(o, me).start()
    idx_all[me] = idx_send[...]

    def taps_of(g):
        taps = taps_ref[pl.ds(pl.multiple_of(g * 16, 16), 16), :]
        return [jnp.broadcast_to(taps[:, j : j + 1], (16, cols)) for j in range(taps_count)]

    def fir(r, at, taps, window):
        total = taps[0] * window[0]
        for j in range(1, taps_count):
            total = total + taps[j] * window[j]
        b, i = r // block_rows, r % block_rows
        z[b, at, i * cols : (i + 1) * cols] = total.astype(BF16)

    @pl.loop(0, dates // 16)
    def _(g):
        taps = taps_of(g)
        for part in range(2):
            at, row = fir_rows(part, g)
            window = [row(r) for r in range(2 * reach)]
            for r in range(reach, rows - reach):
                window = window[-2 * reach :] + [row(r + reach)]
                fir(r, at, taps, window)

    zeros = jnp.zeros((SMOOTH_REACH,) + u.shape[1:], F32)
    u[0:SMOOTH_REACH] = zeros
    u[rows + SMOOTH_REACH : rows + 2 * SMOOTH_REACH] = zeros
    basis = basis_ref[...].astype(F32)
    masked = [jnp.where(window_ref[...] == h, basis, 0.0) for h in range(classes)]
    masked = jnp.concatenate(masked, axis=0)
    masked_ref[...] = masked.astype(BF16)
    spread = []
    for d in range(groups):
        part = masked[:, d * dates : (d + 1) * dates]
        spread += [part, jnp.zeros_like(part)]
    spread_ref[...] = jnp.concatenate(spread, axis=1)
    line = lax.broadcasted_iota(jnp.int32, (classes * bases, 1), 0)
    scales = jnp.ones((classes * bases, 1), F32)
    for h in range(1, classes):
        scales = jnp.where(line >= h * bases, 1.0 / (2 * h + 1), scales)
    line = lax.broadcasted_iota(jnp.int32, order_ref.shape, 0)
    lane = lax.broadcasted_iota(jnp.int32, order_ref.shape, 1)
    whose = jnp.zeros(order_ref.shape, jnp.int32)
    for q in range(1, classes * groups):
        whose = whose + (line >= q * unit).astype(jnp.int32)
    inside = line - whose * unit
    goal = whose * own + (inside >> 1) + (inside & 1) * (classes * bases)
    order_ref[...] = jnp.where((lane == goal) & (inside < 2 * own), 1.0, 0.0).astype(BF16)

    @pl.when(has_low)
    def _():
        halo_up().wait_recv()

    @pl.when(jnp.logical_not(has_low))
    def _():
        halo[0] = jnp.zeros(halo.shape[1:], BF16)

    @pl.when(has_high)
    def _():
        halo_down().wait_recv()

    @pl.when(jnp.logical_not(has_high))
    def _():
        halo[1] = jnp.zeros(halo.shape[1:], BF16)

    @pl.loop(0, dates // 16)
    def _(g):
        taps = taps_of(g)
        for part in range(2):
            at, row = fir_rows(part, g)
            low = [halo[0, q, at, :].astype(F32) for q in range(reach)]
            low += [row(q) for q in range(2 * reach)]
            high = [row(rows - 2 * reach + q) for q in range(2 * reach)]
            high += [halo[1, q, at, :].astype(F32) for q in range(reach)]
            for i in range(reach):
                fir(i, at, taps, low[i : i + taps_count])
                fir(rows - reach + i, at, taps, high[i : i + taps_count])

    def w_copy(o, src):
        return remote(
            wsend.at[peers[o]], what.at[src],
            s_w.at[o], r_w.at[src], peers[o], az,
        )

    for o in list(range(1, groups)) + [0]:
        b = peers[o]
        if o:
            idx_copy(o, b).wait_recv()
        chosen = idx_all[b][0:1, :]
        pixel = lax.broadcasted_iota(jnp.int32, (block_rows * cols, 2 * looks), 0)
        pick = (pixel == chosen).astype(F32).astype(BF16)
        sample = jnp.dot(z[b], pick, preferred_element_type=F32)
        left = lax.broadcasted_iota(jnp.int32, (dates, 2 * looks), 1) < looks
        sample = jnp.where(left, sample[:dates], sample[dates:]).astype(BF16)
        if o:
            wsend[b] = sample
            w_copy(o, me).start()
        else:
            what[me] = sample
    for o in range(1, groups):
        w_copy(o, peers[o]).wait_recv()

    tops = []
    both = []
    for d in range(groups):
        sample = what[d].astype(F32)
        top = jnp.where(left, sample, -sample).astype(BF16)
        tops.append(top)
        both += [top, pltpu.roll(sample, looks, 1).astype(BF16)]
    found = project_gain(
        jnp.concatenate(tops, axis=0), jnp.concatenate(both, axis=0),
        level_ref[...].astype(F32) / 16.0, masked_ref[...], spread_ref[...], scales, looks,
    ).astype(BF16)
    for d in range(groups):
        vsend[d] = found[:, d * 2 * dates : (d + 1) * 2 * dates]

    def v_copy(o, src):
        return remote(vsend.at[peers[o]], vrecv.at[src], s_v.at[o], r_v.at[src], peers[o], az)

    for o in range(1, groups):
        v_copy(o, me).start()
    vrecv[me] = vsend[me]

    def mix_block(b):
        @pl.when(me != b)
        def _():
            v_copy(1, b).wait_recv()

        upper = vrecv[b]
        lower = jnp.concatenate([-upper[:, dates:], upper[:, :dates]], axis=1)
        mix = jnp.dot(
            order_ref[...], jnp.concatenate([upper, lower], axis=0), preferred_element_type=F32
        ).astype(BF16)
        found = jnp.dot(mix, z[b], preferred_element_type=F32)
        for i in range(block_rows):
            u[SMOOTH_REACH + b * block_rows + i] = found[:, i * cols : (i + 1) * cols]

    def smooth(r):
        total = None
        for h in range(classes):
            at = slice(h * groups * unit, (h + 1) * groups * unit)
            for j in range(max(r - h, 0), min(r + h, rows - 1) + 1):
                term = u[j + SMOOTH_REACH, at, :]
                total = term if total is None else total + term
        return total.reshape(groups, unit, cols).astype(BF16)

    def e_copy(side, target):
        return remote(
            esend.at[side], erecv.at[1 - side], s_e.at[side], r_e.at[1 - side], me, target
        )

    mix_block(0)
    for i in range(SMOOTH_REACH):
        esend[0, i] = smooth(i - SMOOTH_REACH)
    pl.when(has_low)(lambda: e_copy(0, az - 1).start())
    mix_block(groups - 1)
    for i in range(SMOOTH_REACH):
        esend[1, i] = smooth(rows + i)
    pl.when(has_high)(lambda: e_copy(1, az + 1).start())
    for b in range(1, groups - 1):
        mix_block(b)

    chunks = (
        pl.ds(block_rows, rows - 2 * block_rows),
        pl.ds(0, block_rows),
        pl.ds(rows - block_rows, block_rows),
    )

    def p_copy(o, src, chunk):
        return remote(
            psend.at[peers[o], chunks[chunk]], precv.at[src, chunks[chunk]],
            s_p.at[chunk, o], r_p.at[chunk, src], peers[o], az,
        )

    def smooth_block(b, d, put):
        first = b * block_rows
        sums = [None] * block_rows
        for h in range(classes):
            at = pl.ds(pl.multiple_of((h * groups + d) * unit, 8), unit)
            terms = [u[first + SMOOTH_REACH + j, at, :] for j in range(-h, block_rows + h)]
            for i in range(block_rows):
                for term in terms[i : i + 2 * h + 1]:
                    sums[i] = term if sums[i] is None else sums[i] + term
        for i in range(block_rows):
            put(first + i, sums[i])

    def put_sent(d):
        def put(r, row):
            psend[d, r] = row.astype(BF16)

        return put

    def put_own(r, row):
        mine[r] = row

    def edge_block(side, d, put):
        first = side * (rows - SMOOTH_REACH)

        def put_edge(r, row):
            if first <= r < first + SMOOTH_REACH:
                row = row + erecv[side, r - first, d].astype(F32)
            put(r, row)

        smooth_block(side * (groups - 1), d, put_edge)

    for o in range(1, groups):

        @pl.loop(1, groups - 1)
        def _(b, o=o):
            smooth_block(b, peers[o], put_sent(peers[o]))

        p_copy(o, me, 0).start()

    @pl.when(has_low)
    def _():
        e_copy(1, az - 1).wait_recv()

    @pl.when(jnp.logical_not(has_low))
    def _():
        erecv[0] = jnp.zeros(erecv.shape[1:], BF16)

    @pl.when(has_high)
    def _():
        e_copy(0, az + 1).wait_recv()

    @pl.when(jnp.logical_not(has_high))
    def _():
        erecv[1] = jnp.zeros(erecv.shape[1:], BF16)

    for o in range(1, groups):
        for side in range(2):
            edge_block(side, peers[o], put_sent(peers[o]))
            p_copy(o, me, 1 + side).start()

    @pl.loop(1, groups - 1)
    def _(b):
        smooth_block(b, me, put_own)

    for side in range(2):
        edge_block(side, me, put_own)

    for chunk in range(3):
        for o in range(1, groups):
            p_copy(o, peers[o], chunk).wait_recv()

    @pl.loop(0, groups)
    def _(b):
        for i in range(block_rows):
            r = b * block_rows + i
            row = mine[r]
            for o in range(1, groups):
                row = row + precv[peers[o], r].astype(F32)
            out_ref[pl.ds(r, 2 * own, stride=rows), :] = row[: 2 * own]

    pl.when(has_low)(lambda: halo_down().wait_send())
    pl.when(has_high)(lambda: halo_up().wait_send())
    for o in range(groups):
        if o:
            idx_copy(o, me).wait_send()
            w_copy(o, me).wait_send()
            v_copy(o, me).wait_send()
            for chunk in range(3):
                p_copy(o, me, chunk).wait_send()
    pl.when(has_low)(lambda: e_copy(0, az - 1).wait_send())
    pl.when(has_high)(lambda: e_copy(1, az + 1).wait_send())


def on_device(slc_stack, fir_taps, look_index, shrink_level, window_half, basis):
    parts, dates, rows, cols = slc_stack.shape
    groups = lax.axis_size("date")
    slabs = lax.axis_size("az")
    taps_count = fir_taps.shape[1]
    looks = look_index.shape[2]
    bases, all_dates = basis.shape
    own = bases // groups
    unit = -(-2 * own // 8) * 8
    classes = SMOOTH_REACH + 1

    pitch = rows + 8

    block_rows = rows // groups
    dma = pltpu.SemaphoreType.DMA
    vmem = pl.BlockSpec(memory_space=pltpu.VMEM)
    scratch = [
        pltpu.VMEM((2 * dates * pitch, cols), F32),
        pltpu.VMEM((2, taps_count // 2, 2 * dates, cols), BF16),
        pltpu.VMEM((2, taps_count // 2, 2 * dates, cols), BF16),
        pltpu.VMEM((8, 2 * looks), jnp.int32),
        pltpu.VMEM((groups, 8, 2 * looks), jnp.int32),
        pltpu.VMEM((classes * bases, all_dates), BF16),
        pltpu.VMEM((classes * bases, 2 * all_dates), F32),
        pltpu.VMEM((classes * groups * unit, 2 * classes * bases), BF16),
        pltpu.VMEM((groups, 2 * dates, block_rows * cols), BF16),
        pltpu.VMEM((groups, dates, 2 * looks), BF16),
        pltpu.VMEM((groups, dates, 2 * looks), BF16),
        pltpu.VMEM((groups, classes * bases, 2 * dates), BF16),
        pltpu.VMEM((groups, classes * bases, 2 * dates), BF16),
        pltpu.VMEM((rows + 2 * SMOOTH_REACH, classes * groups * unit, cols), F32),
        pltpu.VMEM((rows, unit, cols), F32),
        pltpu.VMEM((groups, rows, unit, cols), BF16),
        pltpu.VMEM((groups, rows, unit, cols), BF16),
        pltpu.VMEM((2, SMOOTH_REACH, groups, unit, cols), BF16),
        pltpu.VMEM((2, SMOOTH_REACH, groups, unit, cols), BF16),
        dma((2,)), dma((2,)),
        dma((groups,)), dma((groups,)),
        dma((groups,)), dma((groups,)),
        dma((groups,)), dma((groups,)),
        dma((3, groups)), dma((3, groups)),
        dma((2,)), dma((2,)),
    ]
    out = pl.pallas_call(
        functools.partial(kernel, groups, slabs, unit, own, pitch),
        out_shape=jax.ShapeDtypeStruct((2 * own * rows, cols), F32),
        in_specs=[vmem] * 6,
        out_specs=vmem,
        scratch_shapes=scratch,
        compiler_params=pltpu.CompilerParams(
            collective_id=0, has_side_effects=True, vmem_limit_bytes=60 * 2**20
        ),
    )(
        slc_stack, fir_taps, look_index.reshape(1, looks), shrink_level,
        window_half.reshape(1, all_dates), basis,
    )
    return out.reshape(own, 2, rows, cols)


def solution(mesh):
    in_specs = (
        P(None, "date", "az", None),
        P("date", None),
        P("az", "date", None),
        P("az", "date"),
        P(),
        P(),
    )
    out_specs = P("date", None, "az", None)
    return jax.shard_map(
        on_device, mesh=mesh, in_specs=in_specs, out_specs=out_specs, check_vma=False
    )
```

```python
import functools

import jax
import jax.numpy as jnp
from jax import lax
from jax.experimental import pallas as pl
from jax.experimental.pallas import tpu as pltpu
from jax.sharding import PartitionSpec as P

NS_ITERS = 6
SMOOTH_REACH = 2
MESH = pl.DeviceIdType.MESH
HIGHEST = lax.Precision.HIGHEST
F32 = jnp.float32
BF16 = jnp.bfloat16


def three_terms(array):
    high = array.astype(BF16)
    rest = array - high.astype(F32)
    middle = rest.astype(BF16)
    low = (rest - middle.astype(F32)).astype(BF16)
    return high, middle, low


def exact_dot(left, right):
    l0, l1, l2 = three_terms(left)
    r0, r1, r2 = three_terms(right)
    width = right.shape[1]
    small = jnp.dot(
        jnp.concatenate([l0, l1], axis=1),
        jnp.concatenate(
            [jnp.concatenate([r1, r2], axis=1), jnp.concatenate([r0, r1], axis=1)], axis=0
        ),
        preferred_element_type=F32,
    )
    large = jnp.dot(
        jnp.concatenate([l0, l2], axis=1), jnp.concatenate([r0, r0], axis=0),
        preferred_element_type=F32,
    )
    return large + (small[:, :width] + small[:, width:])


def split_dot(left, right):
    high = left.astype(BF16)
    low = (left - high.astype(F32)).astype(BF16)
    both = lax.dot_general(
        jnp.concatenate([high, low], axis=0), right, (((1,), (1,)), ((), ())),
        preferred_element_type=F32,
    )
    return both[: left.shape[0]] + both[left.shape[0] :]


def project_gain(top, what, weight, masked, spread, scales, looks):
    dates2, width = what.shape
    dates = dates2 // 2
    gram = lax.dot_general(what, what, (((0,), (0,)), ((), ())), preferred_element_type=F32)
    line = lax.broadcasted_iota(jnp.int32, (width, width), 0)
    column = lax.broadcasted_iota(jnp.int32, (width, width), 1)
    eye = (line == column).astype(F32)
    left = lax.broadcasted_iota(jnp.int32, (looks, width), 1) < looks

    def total(array):
        return jnp.sum(jnp.sum(array, axis=1, keepdims=True), axis=0, keepdims=True)

    def full(top):
        turn = pltpu.roll(top, looks, 1)
        return jnp.concatenate([top, jnp.where(left, -turn, turn)], axis=0)

    trace = total(gram * eye) * 0.5
    norm = total(gram * gram) * 0.5
    mu = trace / (looks * dates) + 1e-06
    alpha = (1.0 - weight) / looks
    c = (1.0 + weight) * mu
    core = alpha * gram
    square = alpha * alpha * norm + 2.0 * c * alpha * trace + c * c * dates
    scale = 1.0 / jnp.sqrt(square)
    rho = 1.0 - scale * c
    whole = rho * eye - scale * core
    eye = eye[:looks]
    r = whole[:looks]
    dr = -scale * (rho * eye + r)
    df = -scale * eye
    f0 = 1.0 + rho
    r = exact_dot(r, whole)
    rho = rho * rho
    for step in range(1, NS_ITERS):
        whole = full(r)
        if step == NS_ITERS - 1:
            df = f0 * dr + df + exact_dot(df, whole)
            f0 = f0 * (1.0 + rho)
        elif step == 1:
            out = exact_dot(jnp.concatenate([dr, r], axis=0), whole)
            df = f0 * dr + df - scale * r
            f0 = f0 * (1.0 + rho)
            dr = rho * dr + out[:looks]
            r = out[looks:]
            rho = rho * rho
        else:
            out = exact_dot(jnp.concatenate([df, dr, r], axis=0), whole)
            df = f0 * dr + df + out[:looks]
            f0 = f0 * (1.0 + rho)
            dr = rho * dr + out[looks : 2 * looks]
            r = out[2 * looks :]
            rho = rho * rho
    inner = full(scale * (f0 * eye + weight * mu * df + exact_dot(df, core)))
    base = weight * mu * scale * f0
    seen = jnp.dot(masked, top, preferred_element_type=F32)
    small = exact_dot(alpha * seen, inner)
    return (split_dot(small, what) + base * spread) * scales


def kernel(
    groups, slabs, unit, own, pitch,
    x_ref, taps_ref, look_ref, level_ref, window_ref, basis_ref, out_ref,
    xf, taps_wide, halo_send, halo, idx_send, idx_all, masked_ref, spread_ref, order_ref,
    z, wsend, what, vsend, vrecv, u, mine, psend, precv, esend, erecv,
    s_halo, r_halo, s_idx, r_idx, s_w, r_w, s_v, r_v, s_p, r_p, s_e, r_e,
):
    me = lax.axis_index("date")
    az = lax.axis_index("az")
    _, dates, rows, cols = x_ref.shape
    taps_count = taps_ref.shape[0]
    looks = look_ref.shape[1]
    bases = basis_ref.shape[0]
    block_rows = rows // groups
    reach = taps_count // 2
    classes = SMOOTH_REACH + 1
    has_low = az > 0
    has_high = az < slabs - 1

    barrier = pltpu.get_barrier_semaphore()
    peers = [lax.rem(me + o, groups) for o in range(groups)]

    def greet(d, a):
        pl.semaphore_signal(barrier, inc=1, device_id={"date": d, "az": a}, device_id_type=MESH)

    for o in range(1, groups):
        greet(peers[o], az)

    @pl.when(has_low)
    def _():
        greet(me, az - 1)

    @pl.when(has_high)
    def _():
        greet(me, az + 1)

    chosen = jnp.broadcast_to(look_ref[...], (8, looks))
    idx_send[...] = jnp.concatenate([chosen, chosen], axis=1)

    def widen(t):
        for part in range(2):
            at = pl.ds(pl.multiple_of((part * dates + t) * pitch, 8), rows)
            xf[at, :] = x_ref[part, t].astype(F32)

    @pl.loop(0, dates // 8)
    def _(g):
        for t in range(8):
            widen(g * 8 + t)

    def fir_rows(part, g):
        first = part * dates + g * 16
        return (
            pl.ds(pl.multiple_of(first, 16), 16),
            lambda r: xf[pl.ds(first * pitch + r, 16, stride=pitch), :],
        )

    @pl.loop(0, dates // 16)
    def _(g):
        for part in range(2):
            at, row = fir_rows(part, g)
            for q in range(reach):
                halo_send[0, q, at, :] = row(q).astype(BF16)
                halo_send[1, q, at, :] = row(rows - reach + q).astype(BF16)

    pl.semaphore_wait(
        barrier,
        groups - 1 + has_low.astype(jnp.int32) + has_high.astype(jnp.int32),
    )

    def remote(src, dst, send, recv, d, a):
        return pltpu.make_async_remote_copy(
            src_ref=src, dst_ref=dst, send_sem=send, recv_sem=recv,
            device_id={"date": d, "az": a}, device_id_type=MESH,
        )

    def halo_down():
        return remote(halo_send.at[0], halo.at[1], s_halo.at[0], r_halo.at[1], me, az - 1)

    def halo_up():
        return remote(halo_send.at[1], halo.at[0], s_halo.at[1], r_halo.at[0], me, az + 1)

    def idx_copy(o, src):
        return remote(idx_send, idx_all.at[src], s_idx.at[o], r_idx.at[src], peers[o], az)

    pl.when(has_low)(lambda: halo_down().start())
    pl.when(has_high)(lambda: halo_up().start())
    for o in range(1, groups):
        idx_copy(o, me).start()
    idx_all[me] = idx_send[...]

    line = lax.broadcasted_iota(jnp.int32, (dates, dates), 0)
    column = lax.broadcasted_iota(jnp.int32, (dates, dates), 1)
    for j in range(taps_count):
        own_tap = jnp.where(line == column, taps_ref[j : j + 1, :], 0.0)
        taps_wide[j] = jnp.broadcast_to(jnp.sum(own_tap, axis=1, keepdims=True), (dates, cols))

    def taps_of(g):
        at = pl.ds(pl.multiple_of(g * 16, 16), 16)
        return [taps_wide[j, at, :] for j in range(taps_count)]

    def fir(r, at, taps, window):
        total = taps[0] * window[0]
        for j in range(1, taps_count):
            total = total + taps[j] * window[j]
        b, i = r // block_rows, r % block_rows
        z[b, at, i * cols : (i + 1) * cols] = total.astype(BF16)

    @pl.loop(0, dates // 16)
    def _(g):
        taps = taps_of(g)
        for part in range(2):
            at, row = fir_rows(part, g)
            window = [row(r) for r in range(2 * reach)]
            for r in range(reach, rows - reach):
                window = window[-2 * reach :] + [row(r + reach)]
                fir(r, at, taps, window)

    left = lax.broadcasted_iota(jnp.int32, (dates, 2 * looks), 1) < looks

    def w_copy(b, src):
        return remote(wsend.at[b], what.at[src], s_w.at[b], r_w.at[src], b, az)

    def send_looks(b):
        @pl.when(me != b)
        def _():
            idx_copy(1, b).wait_recv()

        pixel = lax.broadcasted_iota(jnp.int32, (block_rows * cols, 2 * looks), 0)
        pick = (pixel == idx_all[b][0:1, :]).astype(F32).astype(BF16)
        sample = jnp.dot(z[b], pick, preferred_element_type=F32)
        wsend[b] = jnp.where(left, sample[:dates], sample[dates:]).astype(BF16)

        @pl.when(me != b)
        def _():
            w_copy(b, me).start()

        @pl.when(me == b)
        def _():
            what[b] = wsend[b]

    for b in range(1, groups - 1):
        send_looks(b)

    @pl.when(has_low)
    def _():
        halo_up().wait_recv()

    @pl.when(jnp.logical_not(has_low))
    def _():
        halo[0] = jnp.zeros(halo.shape[1:], BF16)

    @pl.when(has_high)
    def _():
        halo_down().wait_recv()

    @pl.when(jnp.logical_not(has_high))
    def _():
        halo[1] = jnp.zeros(halo.shape[1:], BF16)

    @pl.loop(0, dates // 16)
    def _(g):
        taps = taps_of(g)
        for part in range(2):
            at, row = fir_rows(part, g)
            low = [halo[0, q, at, :].astype(F32) for q in range(reach)]
            low += [row(q) for q in range(2 * reach)]
            high = [row(rows - 2 * reach + q) for q in range(2 * reach)]
            high += [halo[1, q, at, :].astype(F32) for q in range(reach)]
            for i in range(reach):
                fir(i, at, taps, low[i : i + taps_count])
                fir(rows - reach + i, at, taps, high[i : i + taps_count])

    send_looks(0)
    send_looks(groups - 1)

    zeros = jnp.zeros((SMOOTH_REACH,) + u.shape[1:], F32)
    u[0:SMOOTH_REACH] = zeros
    u[rows + SMOOTH_REACH : rows + 2 * SMOOTH_REACH] = zeros
    basis = basis_ref[...].astype(F32)
    masked = [jnp.where(window_ref[...] == h, basis, 0.0) for h in range(classes)]
    masked = jnp.concatenate(masked, axis=0)
    masked_ref[...] = masked.astype(BF16)
    spread = []
    for d in range(groups):
        part = masked[:, d * dates : (d + 1) * dates]
        spread += [part, jnp.zeros_like(part)]
    spread_ref[...] = jnp.concatenate(spread, axis=1)
    line = lax.broadcasted_iota(jnp.int32, (classes * bases, 1), 0)
    scales = jnp.ones((classes * bases, 1), F32)
    for h in range(1, classes):
        scales = jnp.where(line >= h * bases, 1.0 / (2 * h + 1), scales)
    line = lax.broadcasted_iota(jnp.int32, order_ref.shape, 0)
    lane = lax.broadcasted_iota(jnp.int32, order_ref.shape, 1)
    whose = jnp.zeros(order_ref.shape, jnp.int32)
    for q in range(1, classes * groups):
        whose = whose + (line >= q * unit).astype(jnp.int32)
    inside = line - whose * unit
    goal = whose * own + (inside >> 1) + (inside & 1) * (classes * bases)
    order_ref[...] = jnp.where((lane == goal) & (inside < 2 * own), 1.0, 0.0).astype(BF16)

    for o in range(1, groups):
        w_copy(peers[o], peers[o]).wait_recv()

    tops = []
    both = []
    for d in range(groups):
        sample = what[d].astype(F32)
        top = jnp.where(left, sample, -sample).astype(BF16)
        tops.append(top)
        both += [top, pltpu.roll(sample, looks, 1).astype(BF16)]
    found = project_gain(
        jnp.concatenate(tops, axis=0), jnp.concatenate(both, axis=0),
        level_ref[...].astype(F32) / 16.0, masked_ref[...], spread_ref[...], scales, looks,
    ).astype(BF16)
    for d in range(groups):
        vsend[d] = found[:, d * 2 * dates : (d + 1) * 2 * dates]

    def v_copy(o, src):
        return remote(vsend.at[peers[o]], vrecv.at[src], s_v.at[o], r_v.at[src], peers[o], az)

    for o in range(1, groups):
        v_copy(o, me).start()
    vrecv[me] = vsend[me]

    def mix_block(b):
        @pl.when(me != b)
        def _():
            v_copy(1, b).wait_recv()

        upper = vrecv[b]
        lower = jnp.concatenate([-upper[:, dates:], upper[:, :dates]], axis=1)
        mix = jnp.dot(
            order_ref[...], jnp.concatenate([upper, lower], axis=0), preferred_element_type=F32
        ).astype(BF16)
        found = jnp.dot(mix, z[b], preferred_element_type=F32)
        for i in range(block_rows):
            u[SMOOTH_REACH + b * block_rows + i] = found[:, i * cols : (i + 1) * cols]

    def smooth(r):
        total = None
        for h in range(classes):
            at = slice(h * groups * unit, (h + 1) * groups * unit)
            for j in range(max(r - h, 0), min(r + h, rows - 1) + 1):
                term = u[j + SMOOTH_REACH, at, :]
                total = term if total is None else total + term
        return total.reshape(groups, unit, cols).astype(BF16)

    def e_copy(side, target):
        return remote(
            esend.at[side], erecv.at[1 - side], s_e.at[side], r_e.at[1 - side], me, target
        )

    mix_block(0)
    for i in range(SMOOTH_REACH):
        esend[0, i] = smooth(i - SMOOTH_REACH)
    pl.when(has_low)(lambda: e_copy(0, az - 1).start())
    mix_block(groups - 1)
    for i in range(SMOOTH_REACH):
        esend[1, i] = smooth(rows + i)
    pl.when(has_high)(lambda: e_copy(1, az + 1).start())
    for b in range(1, groups - 1):
        mix_block(b)

    chunks = (
        pl.ds(block_rows, rows - 2 * block_rows),
        pl.ds(0, block_rows),
        pl.ds(rows - block_rows, block_rows),
    )

    def p_copy(o, src, chunk):
        return remote(
            psend.at[peers[o], chunks[chunk]], precv.at[src, chunks[chunk]],
            s_p.at[chunk, o], r_p.at[chunk, src], peers[o], az,
        )

    def smooth_block(b, d, put):
        first = b * block_rows
        sums = [None] * block_rows
        for h in range(classes):
            at = pl.ds(pl.multiple_of((h * groups + d) * unit, 8), unit)
            terms = [u[first + SMOOTH_REACH + j, at, :] for j in range(-h, block_rows + h)]
            for i in range(block_rows):
                for term in terms[i : i + 2 * h + 1]:
                    sums[i] = term if sums[i] is None else sums[i] + term
        for i in range(block_rows):
            put(first + i, sums[i])

    def put_sent(d):
        def put(r, row):
            psend[d, r] = row.astype(BF16)

        return put

    def put_own(r, row):
        mine[r] = row

    def edge_block(side, d, put):
        first = side * (rows - SMOOTH_REACH)

        def put_edge(r, row):
            if first <= r < first + SMOOTH_REACH:
                row = row + erecv[side, r - first, d].astype(F32)
            put(r, row)

        smooth_block(side * (groups - 1), d, put_edge)

    for o in range(1, groups):

        @pl.loop(1, groups - 1)
        def _(b, o=o):
            smooth_block(b, peers[o], put_sent(peers[o]))

        p_copy(o, me, 0).start()

    @pl.when(has_low)
    def _():
        e_copy(1, az - 1).wait_recv()

    @pl.when(jnp.logical_not(has_low))
    def _():
        erecv[0] = jnp.zeros(erecv.shape[1:], BF16)

    @pl.when(has_high)
    def _():
        e_copy(0, az + 1).wait_recv()

    @pl.when(jnp.logical_not(has_high))
    def _():
        erecv[1] = jnp.zeros(erecv.shape[1:], BF16)

    for o in range(1, groups):
        for side in range(2):
            edge_block(side, peers[o], put_sent(peers[o]))
            p_copy(o, me, 1 + side).start()

    @pl.loop(1, groups - 1)
    def _(b):
        smooth_block(b, me, put_own)

    for side in range(2):
        edge_block(side, me, put_own)

    for chunk in range(3):
        for o in range(1, groups):
            p_copy(o, peers[o], chunk).wait_recv()

    @pl.loop(0, groups)
    def _(b):
        for i in range(block_rows):
            r = b * block_rows + i
            row = mine[r]
            for o in range(1, groups):
                row = row + precv[peers[o], r].astype(F32)
            out_ref[pl.ds(r, 2 * own, stride=rows), :] = row[: 2 * own]

    pl.when(has_low)(lambda: halo_down().wait_send())
    pl.when(has_high)(lambda: halo_up().wait_send())
    for o in range(groups):
        if o:
            idx_copy(o, me).wait_send()
            w_copy(peers[o], me).wait_send()
            v_copy(o, me).wait_send()
            for chunk in range(3):
                p_copy(o, me, chunk).wait_send()
    pl.when(has_low)(lambda: e_copy(0, az - 1).wait_send())
    pl.when(has_high)(lambda: e_copy(1, az + 1).wait_send())


def on_device(slc_stack, fir_taps, look_index, shrink_level, window_half, basis):
    parts, dates, rows, cols = slc_stack.shape
    groups = lax.axis_size("date")
    slabs = lax.axis_size("az")
    taps_count = fir_taps.shape[1]
    looks = look_index.shape[2]
    bases, all_dates = basis.shape
    own = bases // groups
    unit = -(-2 * own // 8) * 8
    classes = SMOOTH_REACH + 1

    pitch = rows + 8

    block_rows = rows // groups
    dma = pltpu.SemaphoreType.DMA
    vmem = pl.BlockSpec(memory_space=pltpu.VMEM)
    scratch = [
        pltpu.VMEM((2 * dates * pitch, cols), F32),
        pltpu.VMEM((taps_count, dates, cols), F32),
        pltpu.VMEM((2, taps_count // 2, 2 * dates, cols), BF16),
        pltpu.VMEM((2, taps_count // 2, 2 * dates, cols), BF16),
        pltpu.VMEM((8, 2 * looks), jnp.int32),
        pltpu.VMEM((groups, 8, 2 * looks), jnp.int32),
        pltpu.VMEM((classes * bases, all_dates), BF16),
        pltpu.VMEM((classes * bases, 2 * all_dates), F32),
        pltpu.VMEM((classes * groups * unit, 2 * classes * bases), BF16),
        pltpu.VMEM((groups, 2 * dates, block_rows * cols), BF16),
        pltpu.VMEM((groups, dates, 2 * looks), BF16),
        pltpu.VMEM((groups, dates, 2 * looks), BF16),
        pltpu.VMEM((groups, classes * bases, 2 * dates), BF16),
        pltpu.VMEM((groups, classes * bases, 2 * dates), BF16),
        pltpu.VMEM((rows + 2 * SMOOTH_REACH, classes * groups * unit, cols), F32),
        pltpu.VMEM((rows, unit, cols), F32),
        pltpu.VMEM((groups, rows, unit, cols), BF16),
        pltpu.VMEM((groups, rows, unit, cols), BF16),
        pltpu.VMEM((2, SMOOTH_REACH, groups, unit, cols), BF16),
        pltpu.VMEM((2, SMOOTH_REACH, groups, unit, cols), BF16),
        dma((2,)), dma((2,)),
        dma((groups,)), dma((groups,)),
        dma((groups,)), dma((groups,)),
        dma((groups,)), dma((groups,)),
        dma((3, groups)), dma((3, groups)),
        dma((2,)), dma((2,)),
    ]
    out = pl.pallas_call(
        functools.partial(kernel, groups, slabs, unit, own, pitch),
        out_shape=jax.ShapeDtypeStruct((2 * own * rows, cols), F32),
        in_specs=[vmem] * 6,
        out_specs=vmem,
        scratch_shapes=scratch,
        compiler_params=pltpu.CompilerParams(
            collective_id=0, has_side_effects=True, vmem_limit_bytes=60 * 2**20
        ),
    )(
        slc_stack, fir_taps.T, look_index.reshape(1, looks), shrink_level,
        window_half.reshape(1, all_dates), basis,
    )
    return out.reshape(own, 2, rows, cols)


def solution(mesh):
    in_specs = (
        P(None, "date", "az", None),
        P("date", None),
        P("az", "date", None),
        P("az", "date"),
        P(),
        P(),
    )
    out_specs = P("date", None, "az", None)
    return jax.shard_map(
        on_device, mesh=mesh, in_specs=in_specs, out_specs=out_specs, check_vma=False
    )
```

```python
import functools

import jax
import jax.numpy as jnp
from jax import lax
from jax.experimental import pallas as pl
from jax.experimental.pallas import tpu as pltpu
from jax.sharding import PartitionSpec as P

NS_ITERS = 6
SMOOTH_REACH = 2
MESH = pl.DeviceIdType.MESH
HIGHEST = lax.Precision.HIGHEST
F32 = jnp.float32
BF16 = jnp.bfloat16


def three_terms(array):
    high = array.astype(BF16)
    rest = array - high.astype(F32)
    middle = rest.astype(BF16)
    low = (rest - middle.astype(F32)).astype(BF16)
    return high, middle, low


def exact_dot(left, right):
    l0, l1, l2 = three_terms(left)
    r0, r1, r2 = three_terms(right)
    width = right.shape[1]
    small = jnp.dot(
        jnp.concatenate([l0, l1], axis=1),
        jnp.concatenate(
            [jnp.concatenate([r1, r2], axis=1), jnp.concatenate([r0, r1], axis=1)], axis=0
        ),
        preferred_element_type=F32,
    )
    large = jnp.dot(
        jnp.concatenate([l0, l2], axis=1), jnp.concatenate([r0, r0], axis=0),
        preferred_element_type=F32,
    )
    return large + (small[:, :width] + small[:, width:])


def split_dot(left, right):
    high = left.astype(BF16)
    low = (left - high.astype(F32)).astype(BF16)
    both = lax.dot_general(
        jnp.concatenate([high, low], axis=0), right, (((1,), (1,)), ((), ())),
        preferred_element_type=F32,
    )
    return both[: left.shape[0]] + both[left.shape[0] :]


def project_gain(top, what, weight, masked, spread, scales, looks):
    dates2, width = what.shape
    dates = dates2 // 2
    gram = lax.dot_general(what, what, (((0,), (0,)), ((), ())), preferred_element_type=F32)
    line = lax.broadcasted_iota(jnp.int32, (width, width), 0)
    column = lax.broadcasted_iota(jnp.int32, (width, width), 1)
    eye = (line == column).astype(F32)
    left = lax.broadcasted_iota(jnp.int32, (looks, width), 1) < looks

    def total(array):
        return jnp.sum(jnp.sum(array, axis=1, keepdims=True), axis=0, keepdims=True)

    def full(top):
        turn = pltpu.roll(top, looks, 1)
        return jnp.concatenate([top, jnp.where(left, -turn, turn)], axis=0)

    trace = total(gram * eye) * 0.5
    norm = total(gram * gram) * 0.5
    mu = trace / (looks * dates) + 1e-06
    alpha = (1.0 - weight) / looks
    c = (1.0 + weight) * mu
    core = alpha * gram
    square = alpha * alpha * norm + 2.0 * c * alpha * trace + c * c * dates
    scale = 1.0 / jnp.sqrt(square)
    rho = 1.0 - scale * c
    whole = rho * eye - scale * core
    eye = eye[:looks]
    r = whole[:looks]
    dr = -scale * (rho * eye + r)
    df = -scale * eye
    f0 = 1.0 + rho
    r = exact_dot(r, whole)
    rho = rho * rho
    for step in range(1, NS_ITERS):
        whole = full(r)
        if step == NS_ITERS - 1:
            df = f0 * dr + df + exact_dot(df, whole)
            f0 = f0 * (1.0 + rho)
        elif step == 1:
            out = exact_dot(jnp.concatenate([dr, r], axis=0), whole)
            df = f0 * dr + df - scale * r
            f0 = f0 * (1.0 + rho)
            dr = rho * dr + out[:looks]
            r = out[looks:]
            rho = rho * rho
        else:
            out = exact_dot(jnp.concatenate([df, dr, r], axis=0), whole)
            df = f0 * dr + df + out[:looks]
            f0 = f0 * (1.0 + rho)
            dr = rho * dr + out[looks : 2 * looks]
            r = out[2 * looks :]
            rho = rho * rho
    inner = full(scale * (f0 * eye + weight * mu * df + exact_dot(df, core)))
    base = weight * mu * scale * f0
    seen = jnp.dot(masked, top, preferred_element_type=F32)
    small = exact_dot(alpha * seen, inner)
    return (split_dot(small, what) + base * spread) * scales


def kernel(
    groups, slabs, unit, own, pitch,
    x_ref, taps_ref, look_ref, level_ref, window_ref, basis_ref, out_ref,
    xf, taps_wide, halo_send, halo, idx_send, idx_all, masked_ref, spread_ref, order_ref,
    z, wsend, what, vsend, vrecv, u, mine, psend, precv, relay, esend, erecv,
    s_halo, r_halo, s_idx, r_idx, s_w, r_w, s_v, r_v, s_p, r_p, r_r, s_e, r_e,
):
    me = lax.axis_index("date")
    az = lax.axis_index("az")
    _, dates, rows, cols = x_ref.shape
    taps_count = taps_ref.shape[0]
    looks = look_ref.shape[1]
    bases = basis_ref.shape[0]
    block_rows = rows // groups
    reach = taps_count // 2
    classes = SMOOTH_REACH + 1
    has_low = az > 0
    has_high = az < slabs - 1

    barrier = pltpu.get_barrier_semaphore()
    peers = [lax.rem(me + o, groups) for o in range(groups)]

    def greet(d, a):
        pl.semaphore_signal(barrier, inc=1, device_id={"date": d, "az": a}, device_id_type=MESH)

    for o in range(1, groups):
        greet(peers[o], az)

    @pl.when(has_low)
    def _():
        greet(me, az - 1)

    @pl.when(has_high)
    def _():
        greet(me, az + 1)

    chosen = jnp.broadcast_to(look_ref[...], (8, looks))
    idx_send[...] = jnp.concatenate([chosen, chosen], axis=1)

    def widen(t):
        for part in range(2):
            at = pl.ds(pl.multiple_of((part * dates + t) * pitch, 8), rows)
            xf[at, :] = x_ref[part, t].astype(F32)

    @pl.loop(0, dates // 8)
    def _(g):
        for t in range(8):
            widen(g * 8 + t)

    def fir_rows(part, g):
        first = part * dates + g * 16
        return (
            pl.ds(pl.multiple_of(first, 16), 16),
            lambda r: xf[pl.ds(first * pitch + r, 16, stride=pitch), :],
        )

    @pl.loop(0, dates // 16)
    def _(g):
        for part in range(2):
            at, row = fir_rows(part, g)
            for q in range(reach):
                halo_send[0, q, at, :] = row(q).astype(BF16)
                halo_send[1, q, at, :] = row(rows - reach + q).astype(BF16)

    pl.semaphore_wait(
        barrier,
        groups - 1 + has_low.astype(jnp.int32) + has_high.astype(jnp.int32),
    )

    def remote(src, dst, send, recv, d, a):
        return pltpu.make_async_remote_copy(
            src_ref=src, dst_ref=dst, send_sem=send, recv_sem=recv,
            device_id={"date": d, "az": a}, device_id_type=MESH,
        )

    def halo_down():
        return remote(halo_send.at[0], halo.at[1], s_halo.at[0], r_halo.at[1], me, az - 1)

    def halo_up():
        return remote(halo_send.at[1], halo.at[0], s_halo.at[1], r_halo.at[0], me, az + 1)

    def idx_copy(o, src):
        return remote(idx_send, idx_all.at[src], s_idx.at[o], r_idx.at[src], peers[o], az)

    pl.when(has_low)(lambda: halo_down().start())
    pl.when(has_high)(lambda: halo_up().start())
    for o in range(1, groups):
        idx_copy(o, me).start()
    idx_all[me] = idx_send[...]

    line = lax.broadcasted_iota(jnp.int32, (dates, dates), 0)
    column = lax.broadcasted_iota(jnp.int32, (dates, dates), 1)
    for j in range(taps_count):
        own_tap = jnp.where(line == column, taps_ref[j : j + 1, :], 0.0)
        taps_wide[j] = jnp.broadcast_to(jnp.sum(own_tap, axis=1, keepdims=True), (dates, cols))

    def taps_of(g):
        at = pl.ds(pl.multiple_of(g * 16, 16), 16)
        return [taps_wide[j, at, :] for j in range(taps_count)]

    def fir(r, at, taps, window):
        total = taps[0] * window[0]
        for j in range(1, taps_count):
            total = total + taps[j] * window[j]
        b, i = r // block_rows, r % block_rows
        z[b, at, i * cols : (i + 1) * cols] = total.astype(BF16)

    @pl.loop(0, dates // 16)
    def _(g):
        taps = taps_of(g)
        for part in range(2):
            at, row = fir_rows(part, g)
            window = [row(r) for r in range(2 * reach)]
            for r in range(reach, rows - reach):
                window = window[-2 * reach :] + [row(r + reach)]
                fir(r, at, taps, window)

    left = lax.broadcasted_iota(jnp.int32, (dates, 2 * looks), 1) < looks

    def w_copy(b, src):
        return remote(wsend.at[b], what.at[src], s_w.at[b], r_w.at[src], b, az)

    def send_looks(b):
        @pl.when(me != b)
        def _():
            idx_copy(1, b).wait_recv()

        pixel = lax.broadcasted_iota(jnp.int32, (block_rows * cols, 2 * looks), 0)
        pick = (pixel == idx_all[b][0:1, :]).astype(F32).astype(BF16)
        sample = jnp.dot(z[b], pick, preferred_element_type=F32)
        wsend[b] = jnp.where(left, sample[:dates], sample[dates:]).astype(BF16)

        @pl.when(me != b)
        def _():
            w_copy(b, me).start()

        @pl.when(me == b)
        def _():
            what[b] = wsend[b]

    for b in range(1, groups - 1):
        send_looks(b)

    @pl.when(has_low)
    def _():
        halo_up().wait_recv()

    @pl.when(jnp.logical_not(has_low))
    def _():
        halo[0] = jnp.zeros(halo.shape[1:], BF16)

    @pl.when(has_high)
    def _():
        halo_down().wait_recv()

    @pl.when(jnp.logical_not(has_high))
    def _():
        halo[1] = jnp.zeros(halo.shape[1:], BF16)

    @pl.loop(0, dates // 16)
    def _(g):
        taps = taps_of(g)
        for part in range(2):
            at, row = fir_rows(part, g)
            low = [halo[0, q, at, :].astype(F32) for q in range(reach)]
            low += [row(q) for q in range(2 * reach)]
            high = [row(rows - 2 * reach + q) for q in range(2 * reach)]
            high += [halo[1, q, at, :].astype(F32) for q in range(reach)]
            for i in range(reach):
                fir(i, at, taps, low[i : i + taps_count])
                fir(rows - reach + i, at, taps, high[i : i + taps_count])

    send_looks(0)
    send_looks(groups - 1)

    zeros = jnp.zeros((SMOOTH_REACH,) + u.shape[1:], F32)
    u[0:SMOOTH_REACH] = zeros
    u[rows + SMOOTH_REACH : rows + 2 * SMOOTH_REACH] = zeros
    basis = basis_ref[...].astype(F32)
    masked = [jnp.where(window_ref[...] == h, basis, 0.0) for h in range(classes)]
    masked = jnp.concatenate(masked, axis=0)
    masked_ref[...] = masked.astype(BF16)
    spread = []
    for d in range(groups):
        part = masked[:, d * dates : (d + 1) * dates]
        spread += [part, jnp.zeros_like(part)]
    spread_ref[...] = jnp.concatenate(spread, axis=1)
    line = lax.broadcasted_iota(jnp.int32, (classes * bases, 1), 0)
    scales = jnp.ones((classes * bases, 1), F32)
    for h in range(1, classes):
        scales = jnp.where(line >= h * bases, 1.0 / (2 * h + 1), scales)
    line = lax.broadcasted_iota(jnp.int32, order_ref.shape, 0)
    lane = lax.broadcasted_iota(jnp.int32, order_ref.shape, 1)
    whose = jnp.zeros(order_ref.shape, jnp.int32)
    for q in range(1, classes * groups):
        whose = whose + (line >= q * unit).astype(jnp.int32)
    inside = line - whose * unit
    goal = whose * own + (inside >> 1) + (inside & 1) * (classes * bases)
    order_ref[...] = jnp.where((lane == goal) & (inside < 2 * own), 1.0, 0.0).astype(BF16)

    for o in range(1, groups):
        w_copy(peers[o], peers[o]).wait_recv()

    tops = []
    both = []
    for d in range(groups):
        sample = what[d].astype(F32)
        top = jnp.where(left, sample, -sample).astype(BF16)
        tops.append(top)
        both += [top, pltpu.roll(sample, looks, 1).astype(BF16)]
    found = project_gain(
        jnp.concatenate(tops, axis=0), jnp.concatenate(both, axis=0),
        level_ref[...].astype(F32) / 16.0, masked_ref[...], spread_ref[...], scales, looks,
    ).astype(BF16)
    for d in range(groups):
        vsend[d] = found[:, d * 2 * dates : (d + 1) * 2 * dates]

    def v_copy(o, src):
        return remote(vsend.at[peers[o]], vrecv.at[src], s_v.at[o], r_v.at[src], peers[o], az)

    for o in range(1, groups):
        v_copy(o, me).start()
    vrecv[me] = vsend[me]

    def mix_block(b):
        @pl.when(me != b)
        def _():
            v_copy(1, b).wait_recv()

        upper = vrecv[b]
        lower = jnp.concatenate([-upper[:, dates:], upper[:, :dates]], axis=1)
        mix = jnp.dot(
            order_ref[...], jnp.concatenate([upper, lower], axis=0), preferred_element_type=F32
        ).astype(BF16)
        found = jnp.dot(mix, z[b], preferred_element_type=F32)
        for i in range(block_rows):
            u[SMOOTH_REACH + b * block_rows + i] = found[:, i * cols : (i + 1) * cols]

    def smooth(r):
        total = None
        for h in range(classes):
            at = slice(h * groups * unit, (h + 1) * groups * unit)
            for j in range(max(r - h, 0), min(r + h, rows - 1) + 1):
                term = u[j + SMOOTH_REACH, at, :]
                total = term if total is None else total + term
        return total.reshape(groups, unit, cols).astype(BF16)

    def e_copy(side, target):
        return remote(
            esend.at[side], erecv.at[1 - side], s_e.at[side], r_e.at[1 - side], me, target
        )

    mix_block(0)
    for i in range(SMOOTH_REACH):
        esend[0, i] = smooth(i - SMOOTH_REACH)
    pl.when(has_low)(lambda: e_copy(0, az - 1).start())
    mix_block(groups - 1)
    for i in range(SMOOTH_REACH):
        esend[1, i] = smooth(rows + i)
    pl.when(has_high)(lambda: e_copy(1, az + 1).start())
    for b in range(1, groups - 1):
        mix_block(b)

    chunks = (
        pl.ds(block_rows, rows - 2 * block_rows),
        pl.ds(0, block_rows),
        pl.ds(rows - block_rows, block_rows),
    )

    def p_copy(o, src, chunk):
        return remote(
            psend.at[peers[o], chunks[chunk]], precv.at[src, chunks[chunk]],
            s_p.at[chunk, o], r_p.at[chunk, src], peers[o], az,
        )

    def smooth_block(b, d, put):
        first = b * block_rows
        sums = [None] * block_rows
        for h in range(classes):
            at = pl.ds(pl.multiple_of((h * groups + d) * unit, 8), unit)
            terms = [u[first + SMOOTH_REACH + j, at, :] for j in range(-h, block_rows + h)]
            for i in range(block_rows):
                for term in terms[i : i + 2 * h + 1]:
                    sums[i] = term if sums[i] is None else sums[i] + term
        for i in range(block_rows):
            put(first + i, sums[i])

    def put_sent(d):
        def put(r, row):
            psend[d, r] = row.astype(BF16)

        return put

    def put_own(r, row):
        mine[r] = row

    def edge_block(side, d, put):
        first = side * (rows - SMOOTH_REACH)

        def put_edge(r, row):
            if first <= r < first + SMOOTH_REACH:
                row = row + erecv[side, r - first, d].astype(F32)
            put(r, row)

        smooth_block(side * (groups - 1), d, put_edge)

    relayed = groups == 4
    at_end = (me == 0) | (me == groups - 1)
    is_far = {1: me == groups - 1, groups - 1: me == 0} if relayed else {}

    def relay_copy(o, chunk):
        return remote(
            psend.at[peers[o], chunks[chunk]], relay.at[chunks[chunk]],
            s_p.at[chunk, o], r_r.at[chunk], jnp.where(me == 0, 1, groups - 2), az,
        )

    def send_part(o, chunk):
        if o in is_far:
            pl.when(is_far[o])(lambda: relay_copy(o, chunk).start())
            pl.when(jnp.logical_not(is_far[o]))(lambda: p_copy(o, me, chunk).start())
        else:
            p_copy(o, me, chunk).start()

    def put_relayed(d):
        def put(r, row):
            psend[d, r] = (row + relay[r].astype(F32)).astype(BF16)

        return put

    direct = list(is_far) if relayed else list(range(1, groups))
    if relayed:

        @pl.when(at_end)
        def _():
            relay[...] = jnp.zeros(relay.shape, BF16)
            precv[groups - 1 - me] = jnp.zeros(precv.shape[1:], BF16)

    for o in direct:

        @pl.loop(1, groups - 1)
        def _(b, o=o):
            smooth_block(b, peers[o], put_sent(peers[o]))

        send_part(o, 0)

    @pl.when(has_low)
    def _():
        e_copy(1, az - 1).wait_recv()

    @pl.when(jnp.logical_not(has_low))
    def _():
        erecv[0] = jnp.zeros(erecv.shape[1:], BF16)

    @pl.when(has_high)
    def _():
        e_copy(0, az + 1).wait_recv()

    @pl.when(jnp.logical_not(has_high))
    def _():
        erecv[1] = jnp.zeros(erecv.shape[1:], BF16)

    for o in direct:
        for side in range(2):
            edge_block(side, peers[o], put_sent(peers[o]))
            send_part(o, 1 + side)

    if relayed:
        last = peers[2]
        for chunk in range(3):

            @pl.when(jnp.logical_not(at_end))
            def _(chunk=chunk):
                relay_copy(2, chunk).wait_recv()

            if chunk == 0:

                @pl.loop(1, groups - 1)
                def _(b):
                    smooth_block(b, last, put_relayed(last))

            else:
                edge_block(chunk - 1, last, put_relayed(last))
            send_part(2, chunk)

    @pl.loop(1, groups - 1)
    def _(b):
        smooth_block(b, me, put_own)

    for side in range(2):
        edge_block(side, me, put_own)

    for chunk in range(3):
        for o in range(1, groups):
            if o in is_far:

                @pl.when(jnp.logical_not(is_far[o]))
                def _(o=o, chunk=chunk):
                    p_copy(o, peers[o], chunk).wait_recv()

            else:
                p_copy(o, peers[o], chunk).wait_recv()

    @pl.loop(0, groups)
    def _(b):
        for i in range(block_rows):
            r = b * block_rows + i
            row = mine[r]
            for o in range(1, groups):
                row = row + precv[peers[o], r].astype(F32)
            out_ref[pl.ds(r, 2 * own, stride=rows), :] = row[: 2 * own]

    pl.when(has_low)(lambda: halo_down().wait_send())
    pl.when(has_high)(lambda: halo_up().wait_send())
    for o in range(groups):
        if o:
            idx_copy(o, me).wait_send()
            w_copy(peers[o], me).wait_send()
            v_copy(o, me).wait_send()
            for chunk in range(3):
                p_copy(o, me, chunk).wait_send()
    pl.when(has_low)(lambda: e_copy(0, az - 1).wait_send())
    pl.when(has_high)(lambda: e_copy(1, az + 1).wait_send())


def on_device(slc_stack, fir_taps, look_index, shrink_level, window_half, basis):
    parts, dates, rows, cols = slc_stack.shape
    groups = lax.axis_size("date")
    slabs = lax.axis_size("az")
    taps_count = fir_taps.shape[1]
    looks = look_index.shape[2]
    bases, all_dates = basis.shape
    own = bases // groups
    unit = -(-2 * own // 8) * 8
    classes = SMOOTH_REACH + 1

    pitch = rows + 8

    block_rows = rows // groups
    dma = pltpu.SemaphoreType.DMA
    vmem = pl.BlockSpec(memory_space=pltpu.VMEM)
    scratch = [
        pltpu.VMEM((2 * dates * pitch, cols), F32),
        pltpu.VMEM((taps_count, dates, cols), F32),
        pltpu.VMEM((2, taps_count // 2, 2 * dates, cols), BF16),
        pltpu.VMEM((2, taps_count // 2, 2 * dates, cols), BF16),
        pltpu.VMEM((8, 2 * looks), jnp.int32),
        pltpu.VMEM((groups, 8, 2 * looks), jnp.int32),
        pltpu.VMEM((classes * bases, all_dates), BF16),
        pltpu.VMEM((classes * bases, 2 * all_dates), F32),
        pltpu.VMEM((classes * groups * unit, 2 * classes * bases), BF16),
        pltpu.VMEM((groups, 2 * dates, block_rows * cols), BF16),
        pltpu.VMEM((groups, dates, 2 * looks), BF16),
        pltpu.VMEM((groups, dates, 2 * looks), BF16),
        pltpu.VMEM((groups, classes * bases, 2 * dates), BF16),
        pltpu.VMEM((groups, classes * bases, 2 * dates), BF16),
        pltpu.VMEM((rows + 2 * SMOOTH_REACH, classes * groups * unit, cols), F32),
        pltpu.VMEM((rows, unit, cols), F32),
        pltpu.VMEM((groups, rows, unit, cols), BF16),
        pltpu.VMEM((groups, rows, unit, cols), BF16),
        pltpu.VMEM((rows, unit, cols), BF16),
        pltpu.VMEM((2, SMOOTH_REACH, groups, unit, cols), BF16),
        pltpu.VMEM((2, SMOOTH_REACH, groups, unit, cols), BF16),
        dma((2,)), dma((2,)),
        dma((groups,)), dma((groups,)),
        dma((groups,)), dma((groups,)),
        dma((groups,)), dma((groups,)),
        dma((3, groups)), dma((3, groups)), dma((3,)),
        dma((2,)), dma((2,)),
    ]
    out = pl.pallas_call(
        functools.partial(kernel, groups, slabs, unit, own, pitch),
        out_shape=jax.ShapeDtypeStruct((2 * own * rows, cols), F32),
        in_specs=[vmem] * 6,
        out_specs=vmem,
        scratch_shapes=scratch,
        compiler_params=pltpu.CompilerParams(
            collective_id=0, has_side_effects=True, vmem_limit_bytes=60 * 2**20
        ),
    )(
        slc_stack, fir_taps.T, look_index.reshape(1, looks), shrink_level,
        window_half.reshape(1, all_dates), basis,
    )
    return out.reshape(own, 2, rows, cols)


def solution(mesh):
    in_specs = (
        P(None, "date", "az", None),
        P("date", None),
        P("az", "date", None),
        P("az", "date"),
        P(),
        P(),
    )
    out_specs = P("date", None, "az", None)
    return jax.shard_map(
        on_device, mesh=mesh, in_specs=in_specs, out_specs=out_specs, check_vma=False
    )
```

```python
import functools

import jax
import jax.numpy as jnp
from jax import lax
from jax.experimental import pallas as pl
from jax.experimental.pallas import tpu as pltpu
from jax.sharding import PartitionSpec as P

NS_ITERS = 6
SMOOTH_REACH = 2
MESH = pl.DeviceIdType.MESH
HIGHEST = lax.Precision.HIGHEST
F32 = jnp.float32
BF16 = jnp.bfloat16


def three_terms(array):
    high = array.astype(BF16)
    rest = array - high.astype(F32)
    middle = rest.astype(BF16)
    low = (rest - middle.astype(F32)).astype(BF16)
    return high, middle, low


def exact_dot(left, right):
    l0, l1, l2 = three_terms(left)
    r0, r1, r2 = three_terms(right)
    width = right.shape[1]
    small = jnp.dot(
        jnp.concatenate([l0, l1], axis=1),
        jnp.concatenate(
            [jnp.concatenate([r1, r2], axis=1), jnp.concatenate([r0, r1], axis=1)], axis=0
        ),
        preferred_element_type=F32,
    )
    large = jnp.dot(
        jnp.concatenate([l0, l2], axis=1), jnp.concatenate([r0, r0], axis=0),
        preferred_element_type=F32,
    )
    return large + (small[:, :width] + small[:, width:])


def split_dot(left, right):
    high = left.astype(BF16)
    low = (left - high.astype(F32)).astype(BF16)
    both = lax.dot_general(
        jnp.concatenate([high, low], axis=0), right, (((1,), (1,)), ((), ())),
        preferred_element_type=F32,
    )
    return both[: left.shape[0]] + both[left.shape[0] :]


def project_gain(top, what, weight, masked, spread, scales, looks):
    dates2, width = what.shape
    dates = dates2 // 2
    gram = lax.dot_general(what, what, (((0,), (0,)), ((), ())), preferred_element_type=F32)
    line = lax.broadcasted_iota(jnp.int32, (width, width), 0)
    column = lax.broadcasted_iota(jnp.int32, (width, width), 1)
    eye = (line == column).astype(F32)
    left = lax.broadcasted_iota(jnp.int32, (looks, width), 1) < looks

    def total(array):
        return jnp.sum(jnp.sum(array, axis=1, keepdims=True), axis=0, keepdims=True)

    def full(top):
        turn = pltpu.roll(top, looks, 1)
        return jnp.concatenate([top, jnp.where(left, -turn, turn)], axis=0)

    trace = total(gram * eye) * 0.5
    norm = total(gram * gram) * 0.5
    mu = trace / (looks * dates) + 1e-06
    alpha = (1.0 - weight) / looks
    c = (1.0 + weight) * mu
    core = alpha * gram
    square = alpha * alpha * norm + 2.0 * c * alpha * trace + c * c * dates
    scale = 1.0 / jnp.sqrt(square)
    rho = 1.0 - scale * c
    whole = rho * eye - scale * core
    eye = eye[:looks]
    r = whole[:looks]
    dr = -scale * (rho * eye + r)
    df = -scale * eye
    f0 = 1.0 + rho
    r = exact_dot(r, whole)
    rho = rho * rho
    for step in range(1, NS_ITERS):
        whole = full(r)
        if step == NS_ITERS - 1:
            df = f0 * dr + df + exact_dot(df, whole)
            f0 = f0 * (1.0 + rho)
        elif step == 1:
            out = exact_dot(jnp.concatenate([dr, r], axis=0), whole)
            df = f0 * dr + df - scale * r
            f0 = f0 * (1.0 + rho)
            dr = rho * dr + out[:looks]
            r = out[looks:]
            rho = rho * rho
        else:
            out = exact_dot(jnp.concatenate([df, dr, r], axis=0), whole)
            df = f0 * dr + df + out[:looks]
            f0 = f0 * (1.0 + rho)
            dr = rho * dr + out[looks : 2 * looks]
            r = out[2 * looks :]
            rho = rho * rho
    inner = full(scale * (f0 * eye + weight * mu * df + exact_dot(df, core)))
    base = weight * mu * scale * f0
    seen = jnp.dot(masked, top, preferred_element_type=F32)
    small = exact_dot(alpha * seen, inner)
    return (split_dot(small, what) + base * spread) * scales


def kernel(
    groups, slabs, unit, own, pitch,
    x_ref, taps_ref, look_ref, level_ref, window_ref, basis_ref, out_ref,
    xf, taps_wide, halo_send, halo, idx_send, idx_all, masked_ref, spread_ref, order_ref,
    z, wsend, what, vsend, vrecv, u, mine, psend, precv, esend, erecv,
    s_halo, r_halo, s_idx, r_idx, s_w, r_w, s_v, r_v, s_p, r_p, s_e, r_e,
):
    me = lax.axis_index("date")
    az = lax.axis_index("az")
    _, dates, rows, cols = x_ref.shape
    taps_count = taps_ref.shape[0]
    looks = look_ref.shape[1]
    bases = basis_ref.shape[0]
    block_rows = rows // groups
    reach = taps_count // 2
    classes = SMOOTH_REACH + 1
    has_low = az > 0
    has_high = az < slabs - 1

    barrier = pltpu.get_barrier_semaphore()
    peers = [lax.rem(me + o, groups) for o in range(groups)]

    def greet(d, a):
        pl.semaphore_signal(barrier, inc=1, device_id={"date": d, "az": a}, device_id_type=MESH)

    for o in range(1, groups):
        greet(peers[o], az)

    @pl.when(has_low)
    def _():
        greet(me, az - 1)

    @pl.when(has_high)
    def _():
        greet(me, az + 1)

    chosen = jnp.broadcast_to(look_ref[...], (8, looks))
    idx_send[...] = jnp.concatenate([chosen, chosen], axis=1)

    def widen(t):
        for part in range(2):
            at = pl.ds(pl.multiple_of((part * dates + t) * pitch, 8), rows)
            xf[at, :] = x_ref[part, t].astype(F32)

    @pl.loop(0, dates // 8)
    def _(g):
        for t in range(8):
            widen(g * 8 + t)

    def fir_rows(part, g):
        first = part * dates + g * 16
        return (
            pl.ds(pl.multiple_of(first, 16), 16),
            lambda r: xf[pl.ds(first * pitch + r, 16, stride=pitch), :],
        )

    @pl.loop(0, dates // 16)
    def _(g):
        for part in range(2):
            at, row = fir_rows(part, g)
            for q in range(reach):
                halo_send[0, q, at, :] = row(q).astype(BF16)
                halo_send[1, q, at, :] = row(rows - reach + q).astype(BF16)

    pl.semaphore_wait(
        barrier,
        groups - 1 + has_low.astype(jnp.int32) + has_high.astype(jnp.int32),
    )

    def remote(src, dst, send, recv, d, a):
        return pltpu.make_async_remote_copy(
            src_ref=src, dst_ref=dst, send_sem=send, recv_sem=recv,
            device_id={"date": d, "az": a}, device_id_type=MESH,
        )

    def halo_down():
        return remote(halo_send.at[0], halo.at[1], s_halo.at[0], r_halo.at[1], me, az - 1)

    def halo_up():
        return remote(halo_send.at[1], halo.at[0], s_halo.at[1], r_halo.at[0], me, az + 1)

    def idx_copy(o, src):
        return remote(idx_send, idx_all.at[src], s_idx.at[o], r_idx.at[src], peers[o], az)

    pl.when(has_low)(lambda: halo_down().start())
    pl.when(has_high)(lambda: halo_up().start())
    for o in range(1, groups):
        idx_copy(o, me).start()
    idx_all[me] = idx_send[...]

    line = lax.broadcasted_iota(jnp.int32, (dates, dates), 0)
    column = lax.broadcasted_iota(jnp.int32, (dates, dates), 1)
    for j in range(taps_count):
        own_tap = jnp.where(line == column, taps_ref[j : j + 1, :], 0.0)
        taps_wide[j] = jnp.broadcast_to(jnp.sum(own_tap, axis=1, keepdims=True), (dates, cols))

    def taps_of(g):
        at = pl.ds(pl.multiple_of(g * 16, 16), 16)
        return [taps_wide[j, at, :] for j in range(taps_count)]

    def fir(r, at, taps, window):
        total = taps[0] * window[0]
        for j in range(1, taps_count):
            total = total + taps[j] * window[j]
        b, i = r // block_rows, r % block_rows
        z[b, at, i * cols : (i + 1) * cols] = total.astype(BF16)

    @pl.loop(0, dates // 16)
    def _(g):
        taps = taps_of(g)
        for part in range(2):
            at, row = fir_rows(part, g)
            window = [row(r) for r in range(2 * reach)]
            for r in range(reach, rows - reach):
                window = window[-2 * reach :] + [row(r + reach)]
                fir(r, at, taps, window)

    left = lax.broadcasted_iota(jnp.int32, (dates, 2 * looks), 1) < looks

    def w_copy(b, src):
        return remote(wsend.at[b], what.at[src], s_w.at[b], r_w.at[src], b, az)

    def send_looks(b):
        @pl.when(me != b)
        def _():
            idx_copy(1, b).wait_recv()

        pixel = lax.broadcasted_iota(jnp.int32, (block_rows * cols, 2 * looks), 0)
        pick = (pixel == idx_all[b][0:1, :]).astype(F32).astype(BF16)
        sample = jnp.dot(z[b], pick, preferred_element_type=F32)
        wsend[b] = jnp.where(left, sample[:dates], sample[dates:]).astype(BF16)

        @pl.when(me != b)
        def _():
            w_copy(b, me).start()

        @pl.when(me == b)
        def _():
            what[b] = wsend[b]

    for b in range(1, groups - 1):
        send_looks(b)

    @pl.when(has_low)
    def _():
        halo_up().wait_recv()

    @pl.when(jnp.logical_not(has_low))
    def _():
        halo[0] = jnp.zeros(halo.shape[1:], BF16)

    @pl.when(has_high)
    def _():
        halo_down().wait_recv()

    @pl.when(jnp.logical_not(has_high))
    def _():
        halo[1] = jnp.zeros(halo.shape[1:], BF16)

    @pl.loop(0, dates // 16)
    def _(g):
        taps = taps_of(g)
        for part in range(2):
            at, row = fir_rows(part, g)
            low = [halo[0, q, at, :].astype(F32) for q in range(reach)]
            low += [row(q) for q in range(2 * reach)]
            high = [row(rows - 2 * reach + q) for q in range(2 * reach)]
            high += [halo[1, q, at, :].astype(F32) for q in range(reach)]
            for i in range(reach):
                fir(i, at, taps, low[i : i + taps_count])
                fir(rows - reach + i, at, taps, high[i : i + taps_count])

    send_looks(0)
    send_looks(groups - 1)

    zeros = jnp.zeros((SMOOTH_REACH,) + u.shape[1:], F32)
    u[0:SMOOTH_REACH] = zeros
    u[rows + SMOOTH_REACH : rows + 2 * SMOOTH_REACH] = zeros
    basis = basis_ref[...].astype(F32)
    masked = [jnp.where(window_ref[...] == h, basis, 0.0) for h in range(classes)]
    masked = jnp.concatenate(masked, axis=0)
    masked_ref[...] = masked.astype(BF16)
    spread = []
    for d in range(groups):
        part = masked[:, d * dates : (d + 1) * dates]
        spread += [part, jnp.zeros_like(part)]
    spread_ref[...] = jnp.concatenate(spread, axis=1)
    line = lax.broadcasted_iota(jnp.int32, (classes * bases, 1), 0)
    scales = jnp.ones((classes * bases, 1), F32)
    for h in range(1, classes):
        scales = jnp.where(line >= h * bases, 1.0 / (2 * h + 1), scales)
    line = lax.broadcasted_iota(jnp.int32, order_ref.shape, 0)
    lane = lax.broadcasted_iota(jnp.int32, order_ref.shape, 1)
    whose = jnp.zeros(order_ref.shape, jnp.int32)
    for q in range(1, classes * groups):
        whose = whose + (line >= q * unit).astype(jnp.int32)
    inside = line - whose * unit
    goal = whose * own + (inside >> 1) + (inside & 1) * (classes * bases)
    order_ref[...] = jnp.where((lane == goal) & (inside < 2 * own), 1.0, 0.0).astype(BF16)

    for o in range(1, groups):
        w_copy(peers[o], peers[o]).wait_recv()

    tops = []
    both = []
    for d in range(groups):
        sample = what[d].astype(F32)
        top = jnp.where(left, sample, -sample).astype(BF16)
        tops.append(top)
        both += [top, pltpu.roll(sample, looks, 1).astype(BF16)]
    found = project_gain(
        jnp.concatenate(tops, axis=0), jnp.concatenate(both, axis=0),
        level_ref[...].astype(F32) / 16.0, masked_ref[...], spread_ref[...], scales, looks,
    ).astype(BF16)
    for d in range(groups):
        vsend[d] = found[:, d * 2 * dates : (d + 1) * 2 * dates]

    def v_copy(o, src):
        return remote(vsend.at[peers[o]], vrecv.at[src], s_v.at[o], r_v.at[src], peers[o], az)

    for o in range(1, groups):
        v_copy(o, me).start()
    vrecv[me] = vsend[me]

    def mix_block(b):
        @pl.when(me != b)
        def _():
            v_copy(1, b).wait_recv()

        upper = vrecv[b]
        lower = jnp.concatenate([-upper[:, dates:], upper[:, :dates]], axis=1)
        mix = jnp.dot(
            order_ref[...], jnp.concatenate([upper, lower], axis=0), preferred_element_type=F32
        ).astype(BF16)
        found = jnp.dot(mix, z[b], preferred_element_type=F32)
        for i in range(block_rows):
            u[SMOOTH_REACH + b * block_rows + i] = found[:, i * cols : (i + 1) * cols]

    def smooth(r):
        total = None
        for h in range(classes):
            at = slice(h * groups * unit, (h + 1) * groups * unit)
            for j in range(max(r - h, 0), min(r + h, rows - 1) + 1):
                term = u[j + SMOOTH_REACH, at, :]
                total = term if total is None else total + term
        return total.reshape(groups, unit, cols).astype(BF16)

    def e_copy(side, target):
        return remote(
            esend.at[side], erecv.at[1 - side], s_e.at[side], r_e.at[1 - side], me, target
        )

    mix_block(0)
    for i in range(SMOOTH_REACH):
        esend[0, i] = smooth(i - SMOOTH_REACH)
    pl.when(has_low)(lambda: e_copy(0, az - 1).start())
    mix_block(groups - 1)
    for i in range(SMOOTH_REACH):
        esend[1, i] = smooth(rows + i)
    pl.when(has_high)(lambda: e_copy(1, az + 1).start())
    for b in range(1, groups - 1):
        mix_block(b)

    chunks = (
        pl.ds(block_rows, rows - 2 * block_rows),
        pl.ds(0, block_rows),
        pl.ds(rows - block_rows, block_rows),
    )

    def p_copy(o, src, chunk):
        return remote(
            psend.at[peers[o], chunks[chunk]], precv.at[src, chunks[chunk]],
            s_p.at[chunk, o], r_p.at[chunk, src], peers[o], az,
        )

    def smooth_block(b, d, put):
        first = b * block_rows
        sums = [None] * block_rows
        for h in range(classes):
            at = pl.ds(pl.multiple_of((h * groups + d) * unit, 8), unit)
            terms = [u[first + SMOOTH_REACH + j, at, :] for j in range(-h, block_rows + h)]
            for i in range(block_rows):
                for term in terms[i : i + 2 * h + 1]:
                    sums[i] = term if sums[i] is None else sums[i] + term
        for i in range(block_rows):
            put(first + i, sums[i])

    def put_sent(d):
        def put(r, row):
            psend[d, r] = row.astype(BF16)

        return put

    def put_own(r, row):
        mine[r] = row

    def edge_block(side, d, put):
        first = side * (rows - SMOOTH_REACH)

        def put_edge(r, row):
            if first <= r < first + SMOOTH_REACH:
                row = row + erecv[side, r - first, d].astype(F32)
            put(r, row)

        smooth_block(side * (groups - 1), d, put_edge)

    far_first = sorted(range(1, groups), key=lambda o: abs(o - groups // 2))
    for o in far_first:

        @pl.loop(1, groups - 1)
        def _(b, o=o):
            smooth_block(b, peers[o], put_sent(peers[o]))

        p_copy(o, me, 0).start()

    @pl.when(has_low)
    def _():
        e_copy(1, az - 1).wait_recv()

    @pl.when(jnp.logical_not(has_low))
    def _():
        erecv[0] = jnp.zeros(erecv.shape[1:], BF16)

    @pl.when(has_high)
    def _():
        e_copy(0, az + 1).wait_recv()

    @pl.when(jnp.logical_not(has_high))
    def _():
        erecv[1] = jnp.zeros(erecv.shape[1:], BF16)

    for o in far_first:
        for side in range(2):
            edge_block(side, peers[o], put_sent(peers[o]))
            p_copy(o, me, 1 + side).start()

    @pl.loop(1, groups - 1)
    def _(b):
        smooth_block(b, me, put_own)

    for side in range(2):
        edge_block(side, me, put_own)

    for chunk in range(3):
        for o in range(1, groups):
            p_copy(o, peers[o], chunk).wait_recv()

    @pl.loop(0, groups)
    def _(b):
        for i in range(block_rows):
            r = b * block_rows + i
            row = mine[r]
            for o in range(1, groups):
                row = row + precv[peers[o], r].astype(F32)
            out_ref[pl.ds(r, 2 * own, stride=rows), :] = row[: 2 * own]

    pl.when(has_low)(lambda: halo_down().wait_send())
    pl.when(has_high)(lambda: halo_up().wait_send())
    for o in range(groups):
        if o:
            idx_copy(o, me).wait_send()
            w_copy(peers[o], me).wait_send()
            v_copy(o, me).wait_send()
            for chunk in range(3):
                p_copy(o, me, chunk).wait_send()
    pl.when(has_low)(lambda: e_copy(0, az - 1).wait_send())
    pl.when(has_high)(lambda: e_copy(1, az + 1).wait_send())


def on_device(slc_stack, fir_taps, look_index, shrink_level, window_half, basis):
    parts, dates, rows, cols = slc_stack.shape
    groups = lax.axis_size("date")
    slabs = lax.axis_size("az")
    taps_count = fir_taps.shape[1]
    looks = look_index.shape[2]
    bases, all_dates = basis.shape
    own = bases // groups
    unit = -(-2 * own // 8) * 8
    classes = SMOOTH_REACH + 1

    pitch = rows + 8

    block_rows = rows // groups
    dma = pltpu.SemaphoreType.DMA
    vmem = pl.BlockSpec(memory_space=pltpu.VMEM)
    scratch = [
        pltpu.VMEM((2 * dates * pitch, cols), F32),
        pltpu.VMEM((taps_count, dates, cols), F32),
        pltpu.VMEM((2, taps_count // 2, 2 * dates, cols), BF16),
        pltpu.VMEM((2, taps_count // 2, 2 * dates, cols), BF16),
        pltpu.VMEM((8, 2 * looks), jnp.int32),
        pltpu.VMEM((groups, 8, 2 * looks), jnp.int32),
        pltpu.VMEM((classes * bases, all_dates), BF16),
        pltpu.VMEM((classes * bases, 2 * all_dates), F32),
        pltpu.VMEM((classes * groups * unit, 2 * classes * bases), BF16),
        pltpu.VMEM((groups, 2 * dates, block_rows * cols), BF16),
        pltpu.VMEM((groups, dates, 2 * looks), BF16),
        pltpu.VMEM((groups, dates, 2 * looks), BF16),
        pltpu.VMEM((groups, classes * bases, 2 * dates), BF16),
        pltpu.VMEM((groups, classes * bases, 2 * dates), BF16),
        pltpu.VMEM((rows + 2 * SMOOTH_REACH, classes * groups * unit, cols), F32),
        pltpu.VMEM((rows, unit, cols), F32),
        pltpu.VMEM((groups, rows, unit, cols), BF16),
        pltpu.VMEM((groups, rows, unit, cols), BF16),
        pltpu.VMEM((2, SMOOTH_REACH, groups, unit, cols), BF16),
        pltpu.VMEM((2, SMOOTH_REACH, groups, unit, cols), BF16),
        dma((2,)), dma((2,)),
        dma((groups,)), dma((groups,)),
        dma((groups,)), dma((groups,)),
        dma((groups,)), dma((groups,)),
        dma((3, groups)), dma((3, groups)),
        dma((2,)), dma((2,)),
    ]
    out = pl.pallas_call(
        functools.partial(kernel, groups, slabs, unit, own, pitch),
        out_shape=jax.ShapeDtypeStruct((2 * own * rows, cols), F32),
        in_specs=[vmem] * 6,
        out_specs=vmem,
        scratch_shapes=scratch,
        compiler_params=pltpu.CompilerParams(
            collective_id=0, has_side_effects=True, vmem_limit_bytes=60 * 2**20
        ),
    )(
        slc_stack, fir_taps.T, look_index.reshape(1, looks), shrink_level,
        window_half.reshape(1, all_dates), basis,
    )
    return out.reshape(own, 2, rows, cols)


def solution(mesh):
    in_specs = (
        P(None, "date", "az", None),
        P("date", None),
        P("az", "date", None),
        P("az", "date"),
        P(),
        P(),
    )
    out_specs = P("date", None, "az", None)
    return jax.shard_map(
        on_device, mesh=mesh, in_specs=in_specs, out_specs=out_specs, check_vma=False
    )
```
